32 devices in a mesh: seq: 4 (over y, x), expert: 8 (over z, core).
Axes of the slice: x: 2, y: 2, z: 4, core: 2. Of those that a mesh axis runs over, the one named last changes fastest.
Arguments:
- tokens: bfloat16 [512, 2048], P(('seq', 'expert')), may hold values from -6 to 6
- out_grads: bfloat16 [512, 2048], P(('seq', 'expert')), may hold values from -6 to 6
- route_ids: int32 [512, 6], P(('seq', 'expert')), may hold values from 0 to 15, all different within a row; in each aligned block of 16 rows (0 to 15, 16 to 31, ...) at most 8 rows name the same one
- route_probs: bfloat16 [512, 6], P(('seq', 'expert')), may hold values from 0.049804688 to 1
- w_gate_up: bfloat16 [32, 2, 704, 2048], P(('seq', 'expert')), may hold values from -0.125 to 0.125
- w_down: bfloat16 [32, 704, 2048], P(('seq', 'expert')), may hold values from -0.15625 to 0.15625
Outputs:
- grad_tokens: bfloat16 [512, 2048], P(('seq', 'expert'))
- grad_probs: float32 [512, 6], P(('seq', 'expert'))
- grad_gate_up: bfloat16 [32, 2, 704, 2048], P(('seq', 'expert'))
- grad_down: bfloat16 [32, 704, 2048], P(('seq', 'expert'))
The draws below stay inside these ranges and needn't reach their ends.
Inputs may be any that keep to these rules, and one draw needn't show every extreme that they name: `route_ids`: in the rows of one device (16 aligned rows) no expert is named by more than 8 routes, a bound that some block reaches; a token's 6 experts differ.
All inputs are finite; a program needn't handle non-finite values.
Results may differ from the reference program's by a relative error of at most 0.0065.
Values may be sent and summed in bfloat16 or wider, within the bound.
No kernel may reach another device: no remote copies, remote signals or barrier semaphores. Data moves between devices by JAX's collectives and lax.ppermute only.
A program may use at most 64 MiB of HBM per device.

```python
import math
import jax
import jax.numpy as jnp
import numpy as np
from jax import lax

D = 2048
FF = 1408
TOP = 6
TOK_DEV = 16
SLICES = 2
HID_DEV = 704
EXPERTS = 16
CAP = 8
TOKENS = 512


def block_levels(own_key, extent, shards, least, largest):
    def one(axis_at, parts):
        draws = jax.random.uniform(jax.random.fold_in(jax.random.fold_in(own_key, 6), axis_at), (parts,), jnp.float32, least / len(shards), largest / len(shards))
        return jnp.repeat(jnp.exp(draws), extent[axis_at] // parts).reshape((-1,) + (1,) * (len(extent) - axis_at - 1))

    factor_of = one(*shards[0])
    for cut in shards[1:]:
        factor_of = factor_of * one(*cut)
    return factor_of


def routed_block(rng, own, number, rows, count, top, limit, lean):
    sequence = jax.random.permutation(rng, count)
    crowded, ordinary = shares(count, rows * top, limit, lean, True), shares(count, rows * top, limit, lean, False)
    places = jnp.arange(count)

    def named(sizes, turn):
        used = int((sizes > 0).sum())
        fixed = max(1, used // 4)
        shifted = fixed + (places - fixed + turn * (used - fixed)) % max(1, count - fixed)
        return jnp.zeros((count,), jnp.int32).at[sequence[jnp.where(places < fixed, places, shifted)]].set(jnp.asarray(sizes, jnp.int32))

    sizes = jnp.where(number % 4 == 0, named(crowded, number // 4), named(ordinary, number - number // 4 - 1))
    mixed = jax.random.permutation(jax.random.fold_in(own, 3), count)
    giver, sink = mixed[0:count // 2 * 2:2], mixed[1:count // 2 * 2:2]
    margin = jnp.minimum(sizes[giver] - 1, limit - sizes[sink]) // 2
    margin = jnp.where((giver == sequence[0]) | (sink == sequence[0]) | (sizes[sink] == 0), 0, jnp.maximum(margin, 0))
    shifted = jax.random.randint(jax.random.fold_in(own, 4), (count // 2,), 0, 1 << 20) % (margin + 1)
    sizes = sizes.at[giver].add(-shifted).at[sink].add(shifted)
    items = jnp.searchsorted(jnp.cumsum(sizes), jnp.arange(rows * top), side="right").astype(jnp.int32)
    listing = items.reshape(top, rows).T
    listing = listing[jax.random.permutation(jax.random.fold_in(own, 1), rows)]
    turn = jax.random.randint(jax.random.fold_in(own, 2), (rows, 1), 0, top)
    return jnp.take_along_axis(listing, (jnp.arange(top)[None, :] + turn) % top, axis=1)


def shares(number_of, total, most, skew, full):
    portions = [(1 << 20) // math.isqrt(standing ** skew) + 1 for standing in range(1, number_of + 1)]
    largest = most if full else min(most, max(-(-total // number_of), total * portions[0] // sum(portions)))
    least = 1 if total - largest >= number_of - 1 else 0
    given, surplus = [largest] + [least] * (number_of - 1), total - largest - least * (number_of - 1)
    while surplus > 0:
        free = [i for i in range(1, number_of) if given[i] < largest] or [i for i in range(1, number_of) if given[i] < most]
        whole, remaining = sum([portions[i] for i in free]), surplus
        for i in free:
            more = min(most - given[i], max(1, remaining * portions[i] // whole), surplus)
            given[i] = given[i] + more
            surplus = surplus - more
    return np.array(given)


def normal_values(key, shape, spread, bound, pieces=(), kind=jnp.bfloat16):
    loudness = block_levels(key, shape, pieces, -0.22, 0.18) if pieces else 1.0
    entries = jax.random.normal(key, shape, jnp.float32) * spread * loudness
    return jnp.minimum(jnp.maximum(entries, -bound), bound).astype(kind)


def setup_inputs(seed: int = 0) -> dict:
    streams_of = jax.random.split(jax.random.key(seed), 7)
    tokens = normal_values(streams_of[0], (TOKENS, D), 1.0, 6.0, ((0, 32),))
    out_grads = normal_values(streams_of[1], (TOKENS, D), 1.0, 6.0, ((0, 32),))
    route_ids_keys = jax.random.split(jax.random.fold_in(streams_of[2], 1), TOKENS // TOK_DEV)
    route_ids_turns = jax.random.permutation(jax.random.fold_in(streams_of[2], 3), TOKENS // TOK_DEV)
    route_ids = jax.vmap(lambda own, number: routed_block(jax.random.fold_in(streams_of[2], 2), own, number, TOK_DEV, EXPERTS, TOP, CAP, 2))(route_ids_keys, route_ids_turns).reshape((TOKENS, TOP))
    route_probs = jnp.clip(jnp.exp(math.log(1.0) - 2.9996462 * jax.random.uniform(streams_of[3], (TOKENS, TOP), jnp.float32) ** block_levels(streams_of[3], (TOKENS, TOP), ((0, 32),), -0.2, 0.2)), 0.049804688, 1.0).astype(jnp.bfloat16)
    w_gate_up = normal_values(streams_of[4], (EXPERTS * SLICES, 2, HID_DEV, D), D ** -0.5, 0.125, ((0, 32),))
    w_down = normal_values(streams_of[5], (EXPERTS * SLICES, HID_DEV, D), FF ** -0.5, 0.15625, ((0, 32),))
    return dict(tokens=tokens, out_grads=out_grads, route_ids=route_ids, route_probs=route_probs, w_gate_up=w_gate_up, w_down=w_down)


def slot_numbers(route_ids):
    nrows = route_ids.shape[0]
    blocks = nrows // TOK_DEV
    flat = route_ids.reshape(blocks, TOK_DEV * TOP)
    onehot = (flat[:, :, None] == jnp.arange(EXPERTS, dtype=jnp.int32)[None, None, :]).astype(jnp.int32)
    before = jnp.cumsum(onehot, axis=1) - onehot
    rank = jnp.sum(before * onehot, axis=2)
    slot = jnp.arange(blocks, dtype=jnp.int32)[:, None] * CAP + rank
    return slot.reshape(nrows, TOP).astype(jnp.int32)


def rounded(value):
    return lax.optimization_barrier(value.astype(jnp.bfloat16)).astype(jnp.float32)


def reference(tokens, out_grads, route_ids, route_probs, w_gate_up, w_down):
    nrows = tokens.shape[0]
    nroutes = nrows * TOP
    slot = slot_numbers(route_ids)
    slots_all = (nrows // TOK_DEV) * CAP
    table = jnp.full((EXPERTS, slots_all), nroutes, dtype=jnp.int32)
    table = table.at[route_ids.reshape(-1), slot.reshape(-1)].set(jnp.arange(nroutes, dtype=jnp.int32))
    tokens_pad = jnp.concatenate([tokens, jnp.zeros((1, D), tokens.dtype)], 0)
    grads_pad = jnp.concatenate([out_grads, jnp.zeros((1, D), out_grads.dtype)], 0)
    probs_pad = jnp.concatenate([route_probs.reshape(-1), jnp.zeros((1,), route_probs.dtype)], 0)
    gate_up_all = w_gate_up.reshape(EXPERTS, SLICES, 2, HID_DEV, D)
    down_all = w_down.reshape(EXPERTS, SLICES, HID_DEV, D)

    def expert_grads(packed):
        index, gate_up, down = packed
        token = (index // TOP).astype(jnp.int32)
        xs = tokens_pad[token]
        dys = grads_pad[token]
        weight = probs_pad[index].astype(jnp.float32)[:, None]
        scaled = (weight * dys.astype(jnp.float32)).astype(jnp.bfloat16)
        dx_total = jnp.zeros((slots_all, D), jnp.float32)
        score_total = jnp.zeros((slots_all,), jnp.float32)
        gate_parts, up_parts, down_parts = [], [], []
        for part in range(SLICES):
            w_gate = gate_up[part, 0]
            w_up = gate_up[part, 1]
            w_out = down[part]
            gate = jnp.dot(xs, w_gate.T, preferred_element_type=jnp.float32)
            upper = jnp.dot(xs, w_up.T, preferred_element_type=jnp.float32)
            sig = jax.nn.sigmoid(gate)
            act = gate * sig * upper
            err = jnp.dot(dys, w_out.T, preferred_element_type=jnp.float32)
            score_total = score_total + rounded(jnp.sum(err * act, axis=1))
            delta = weight * err
            grad_g = (delta * upper * sig * (1.0 + gate * (1.0 - sig))).astype(jnp.bfloat16)
            grad_u = (delta * gate * sig).astype(jnp.bfloat16)
            dx_part = jnp.dot(grad_g, w_gate, preferred_element_type=jnp.float32) + jnp.dot(grad_u, w_up, preferred_element_type=jnp.float32)
            dx_total = dx_total + rounded(dx_part)
            gate_parts.append(jnp.dot(grad_g.T, xs, preferred_element_type=jnp.float32).astype(jnp.bfloat16))
            up_parts.append(jnp.dot(grad_u.T, xs, preferred_element_type=jnp.float32).astype(jnp.bfloat16))
            down_parts.append(jnp.dot(act.astype(jnp.bfloat16).T, scaled, preferred_element_type=jnp.float32).astype(jnp.bfloat16))
        grad_gu = jnp.stack([jnp.stack(gate_parts, 0), jnp.stack(up_parts, 0)], 1)
        return dx_total.astype(jnp.bfloat16), score_total.astype(jnp.bfloat16), grad_gu, jnp.stack(down_parts, 0)

    slot_dx, slot_score, grad_gate_up, grad_down = lax.map(expert_grads, (table, gate_up_all, down_all))
    total = jnp.zeros((nrows, D), jnp.float32)
    for pick in range(TOP):
        total = total + slot_dx[route_ids[:, pick], slot[:, pick]].astype(jnp.float32)
    grad_probs = slot_score[route_ids, slot].astype(jnp.float32)
    grad_gate_up = grad_gate_up.reshape(EXPERTS * SLICES, 2, HID_DEV, D)
    grad_down = grad_down.reshape(EXPERTS * SLICES, HID_DEV, D)
    return total.astype(jnp.bfloat16), grad_probs, grad_gate_up, grad_down
```

```python
import jax
import jax.numpy as jnp
from jax import lax
from jax.experimental import pallas as pl
from jax.experimental.pallas import tpu as pltpu
from jax.sharding import Mesh
from jax.sharding import PartitionSpec as P

LANES = 128
LIMIT = 50 * 1024 * 1024
F32, BF16 = jnp.float32, jnp.bfloat16


def dot(a, b, ca, cb):
    return lax.dot_general(a, b, (((ca,), (cb,)), ((), ())), preferred_element_type=F32)


def slot_table(ids, capacity, slots):
    rows, top = ids.shape
    lane = lax.broadcasted_iota(jnp.int32, (rows, slots), 1)
    expert, place = lane // capacity, lane % capacity
    named = jnp.zeros((rows, slots), F32)
    for k in range(top):
        named = named + (ids[:, k : k + 1] == expert).astype(F32)
    earlier = lax.broadcasted_iota(jnp.int32, (rows, rows), 1) < lax.broadcasted_iota(
        jnp.int32, (rows, rows), 0
    )
    rank = dot(earlier.astype(BF16), named.astype(BF16), 1, 0)
    held = jnp.where(rank == place.astype(F32), named, 0.0)
    return expert, held


def pack_kernel(capacity, x_ref, dy_ref, ids_ref, p_ref, out_ref):
    slots, width = out_ref.shape[0], x_ref.shape[1]
    ids = ids_ref[...]
    expert, held = slot_table(ids, capacity, slots)
    probs = p_ref[...].astype(F32)
    weight = jnp.zeros(held.shape, F32)
    for k in range(ids.shape[1]):
        weight = weight + jnp.where(ids[:, k : k + 1] == expert, probs[:, k : k + 1], 0.0)
    pick = held.astype(BF16)
    out_ref[:, :width] = dot(pick, x_ref[...], 0, 0).astype(BF16)
    out_ref[:, width : 2 * width] = dot(pick, dy_ref[...], 0, 0).astype(BF16)
    ones = jnp.ones((ids.shape[0], LANES), BF16)
    out_ref[:, 2 * width :] = dot((held * weight).astype(BF16), ones, 0, 0).astype(BF16)


def main_kernel(parts, *refs):
    got = refs[:parts]
    wgu_hbm, wd_hbm = refs[parts : parts + 2]
    dx_out = refs[parts + 2 : 2 * parts + 2]
    gg_ref, gu_ref, act_ref, x_out, scaled_ref = refs[2 * parts + 2 : 2 * parts + 7]
    rows_ref, wg, wu, wd, sems = refs[2 * parts + 7 :]
    slots, width = got[0].shape[0], wg.shape[1]
    row_copies = [
        pltpu.make_async_copy(got[i], rows_ref.at[pl.ds(i * slots, slots)], sems.at[3 + i])
        for i in range(parts)
    ]
    w_copies = [
        pltpu.make_async_copy(wgu_hbm.at[0, 0], wg, sems.at[0]),
        pltpu.make_async_copy(wgu_hbm.at[0, 1], wu, sems.at[1]),
        pltpu.make_async_copy(wd_hbm.at[0], wd, sems.at[2]),
    ]
    for c in row_copies:
        c.start()
    for c in w_copies:
        c.start()
    for c in row_copies:
        c.wait()
    w_copies[0].wait()
    gate = dot(wg[...], rows_ref[:, :width], 1, 1)
    w_copies[1].wait()
    upper = dot(wu[...], rows_ref[:, :width], 1, 1)
    w_copies[2].wait()
    err = dot(wd[...], rows_ref[:, width : 2 * width], 1, 1)
    weight_col = rows_ref[:, 2 * width :].astype(F32)
    weight = jnp.transpose(weight_col)[0:1, :]
    sig = jax.nn.sigmoid(gate)
    silu = gate * sig
    act = silu * upper
    score = jnp.sum(err * act, axis=0, keepdims=True)
    delta = weight * err
    gg = (delta * upper * sig * (1.0 + gate * (1.0 - sig))).astype(BF16)
    gu = (delta * silu).astype(BF16)
    gg_ref[...] = gg
    gu_ref[...] = gu
    act_ref[...] = act.astype(BF16)
    score_col = jnp.transpose(jnp.broadcast_to(score, (LANES, score.shape[1]))).astype(BF16)
    dx = (dot(gg, wg[...], 0, 0) + dot(gu, wu[...], 0, 0)).astype(BF16)
    for i in range(parts):
        dx_out[i][:, :width] = dx[i * slots : (i + 1) * slots]
        dx_out[i][:, width:] = score_col[i * slots : (i + 1) * slots]
    x_out[...] = rows_ref[:, :width]
    dys = rows_ref[:, width : 2 * width].astype(F32)
    scaled_ref[...] = (weight_col[:, 0:1] * dys).astype(BF16)


def weights_kernel(gg_ref, gu_ref, act_ref, x_ref, scaled_ref, dgu_hbm, dd_hbm, buf, sems):
    copies = [
        pltpu.make_async_copy(buf.at[0], dgu_hbm.at[0, 0], sems.at[0]),
        pltpu.make_async_copy(buf.at[1], dgu_hbm.at[0, 1], sems.at[1]),
        pltpu.make_async_copy(buf.at[2], dd_hbm.at[0], sems.at[2]),
    ]
    for i, (lhs, rhs) in enumerate(((gg_ref, x_ref), (gu_ref, x_ref), (act_ref, scaled_ref))):
        buf[i] = dot(lhs[...], rhs[...], 1, 0).astype(BF16)
        copies[i].start()
    for c in copies:
        c.wait()


def add_kernel(parts, *refs):
    total = refs[0][...].astype(F32)
    for r in refs[1:parts]:
        total = total + r[...].astype(F32)
    refs[parts][...] = total.astype(BF16)


def final_kernel(capacity, back_ref, ids_ref, dx_ref, dp_ref):
    slots, width = back_ref.shape[0], dx_ref.shape[1]
    ids = ids_ref[...]
    rows, top = ids.shape
    expert, held = slot_table(ids, capacity, slots)
    dx_ref[...] = dot(held.astype(BF16), back_ref[:, :width], 1, 0).astype(BF16)
    score = back_ref[:, width:]
    lane = lax.broadcasted_iota(jnp.int32, (rows, LANES), 1)
    probs = jnp.zeros((rows, LANES), F32)
    for k in range(top):
        mine = jnp.where(ids[:, k : k + 1] == expert, held, 0.0).astype(BF16)
        probs = jnp.where(lane == k, dot(mine, score, 1, 0), probs)
    dp_ref[...] = probs[:, :top]


def params():
    return pltpu.CompilerParams(vmem_limit_bytes=LIMIT)


VMEM = pl.BlockSpec(memory_space=pltpu.VMEM)
ANY = pl.BlockSpec(memory_space=pl.ANY)


def body(tokens, out_grads, route_ids, route_probs, w_gate_up, w_down):
    rows, width = tokens.shape
    top = route_ids.shape[1]
    groups, deep, parts = lax.axis_size("seq"), lax.axis_size("z"), lax.axis_size("slice")
    experts = groups * deep
    hidden = w_down.shape[1]
    capacity = max(2, (rows * top * 4 // 3 + experts - 1) // experts)
    slots = experts * capacity
    total = slots * parts

    def everywhere(v):
        return lax.all_to_all(
            v.reshape(experts, capacity, v.shape[1]),
            ("seq", "z"),
            split_axis=0,
            concat_axis=0,
            tiled=True,
        ).reshape(v.shape)

    def across(v, step):
        return lax.ppermute(v, "slice", [(i, (i + step) % parts) for i in range(parts)])

    packed = pl.pallas_call(
        lambda *r: pack_kernel(capacity, *r),
        out_shape=jax.ShapeDtypeStruct((slots, 2 * width + LANES), BF16),
        in_specs=[VMEM] * 4,
        out_specs=VMEM,
        compiler_params=params(),
        name="pack",
    )(tokens, out_grads, route_ids, route_probs)
    mine = everywhere(packed)
    got = [mine] + [across(mine, i) for i in range(1, parts)]

    sd = jax.ShapeDtypeStruct
    outs = pl.pallas_call(
        lambda *r: main_kernel(parts, *r),
        out_shape=[sd((slots, width + LANES), BF16)] * parts
        + [sd((hidden, total), BF16)] * 3
        + [sd((total, width), BF16)] * 2,
        in_specs=[ANY] * (parts + 2),
        out_specs=[VMEM] * (parts + 5),
        scratch_shapes=[
            pltpu.VMEM((total, 2 * width + LANES), BF16),
            pltpu.VMEM((hidden, width), BF16),
            pltpu.VMEM((hidden, width), BF16),
            pltpu.VMEM((hidden, width), BF16),
            pltpu.SemaphoreType.DMA((3 + parts,)),
        ],
        compiler_params=params(),
        name="expert",
    )(*got, w_gate_up, w_down)
    dx_parts, (gg, gu, act, xs, scaled) = outs[:parts], outs[parts:]
    returned = [dx_parts[0]] + [across(dx_parts[i], -i) for i in range(1, parts)]
    summed = pl.pallas_call(
        lambda *r: add_kernel(parts, *r),
        out_shape=sd((slots, width + LANES), BF16),
        in_specs=[VMEM] * parts,
        out_specs=VMEM,
        compiler_params=params(),
        name="add",
    )(*returned)
    back = everywhere(summed)
    grad_gu, grad_down = pl.pallas_call(
        weights_kernel,
        out_shape=[sd(w_gate_up.shape, BF16), sd(w_down.shape, BF16)],
        in_specs=[VMEM] * 5,
        out_specs=[ANY] * 2,
        scratch_shapes=[
            pltpu.VMEM((3, hidden, width), BF16),
            pltpu.SemaphoreType.DMA((3,)),
        ],
        compiler_params=params(),
        cost_estimate=pl.CostEstimate(
            flops=6 * hidden * total * width,
            bytes_accessed=10 * hidden * width,
            transcendentals=0,
        ),
        name="weights",
    )(gg, gu, act, xs, scaled)
    grad_tokens, grad_probs = pl.pallas_call(
        lambda *r: final_kernel(capacity, *r),
        out_shape=[sd((rows, width), BF16), sd((rows, top), F32)],
        in_specs=[VMEM] * 2,
        out_specs=[VMEM] * 2,
        compiler_params=params(),
        name="final",
    )(back, route_ids)
    return grad_tokens, grad_probs, grad_gu, grad_down


def solution(mesh):
    groups, columns = mesh.devices.shape
    split = Mesh(mesh.devices.reshape(groups, 4, columns // 4), ("seq", "z", "slice"))
    every = ("seq", "z", "slice")

    def spec(rank):
        return P(every, *([None] * (rank - 1)))

    return jax.shard_map(
        body,
        mesh=split,
        in_specs=(spec(2), spec(2), spec(2), spec(2), spec(4), spec(3)),
        out_specs=(spec(2), spec(2), spec(4), spec(3)),
        check_vma=False,
    )
```

```python
import jax
import jax.numpy as jnp
from jax import lax
from jax.experimental import pallas as pl
from jax.experimental.pallas import tpu as pltpu
from jax.sharding import Mesh
from jax.sharding import PartitionSpec as P

LANES = 128
F32, BF16 = jnp.float32, jnp.bfloat16


def dot(a, b, ca, cb):
    return lax.dot_general(a, b, (((ca,), (cb,)), ((), ())), preferred_element_type=F32)


def lane_map(count, start):
    row = lax.broadcasted_iota(jnp.int32, (count, LANES), 0)
    lane = lax.broadcasted_iota(jnp.int32, (count, LANES), 1)
    return (lane == row + start).astype(BF16)


def slot_table(meta, top, upper_half, which, capacity, slots):
    rows = meta.shape[0]
    lane = lax.broadcasted_iota(jnp.int32, (rows, slots), 1)
    device = lane // (2 * capacity)
    expert = ((device // 2) * 4 + upper_half * 2 + device % 2).astype(F32)
    mine = (lane // capacity) % 2 == which
    place = (lane % capacity).astype(F32)
    match = [meta[:, k : k + 1] == expert for k in range(top)]
    named = jnp.zeros((rows, slots), F32)
    for m in match:
        named = named + m.astype(F32)
    earlier = lax.broadcasted_iota(jnp.int32, (rows, rows), 1) < lax.broadcasted_iota(
        jnp.int32, (rows, rows), 0
    )
    rank = dot(earlier.astype(BF16), named.astype(BF16), 1, 0)
    held = jnp.where(mine & (rank == place), named, 0.0)
    return match, held


def pack_kernel(x_hbm, dy_hbm, ids_ref, p_ref, out_ref, sems):
    width, top = x_hbm.shape[1], ids_ref.shape[0]
    copies = [
        pltpu.make_async_copy(x_hbm, out_ref.at[:, pl.ds(0, width)], sems.at[0]),
        pltpu.make_async_copy(dy_hbm, out_ref.at[:, pl.ds(width, width)], sems.at[1]),
    ]
    for c in copies:
        c.start()
    ids = ids_ref[...].astype(F32).astype(BF16)
    meta = dot(ids, lane_map(top, 0), 0, 0) + dot(p_ref[...], lane_map(top, top), 0, 0)
    out_ref[:, 2 * width :] = meta.astype(BF16)
    for c in copies:
        c.wait()


def select_kernel(top, capacity, half_ref, own_ref, far_ref, out_ref):
    slots, width = out_ref.shape[0], (out_ref.shape[1] - LANES) // 2
    picks, weighted = [], []
    for which, ref in enumerate((own_ref, far_ref)):
        meta = ref[:, 2 * width :].astype(F32)
        match, held = slot_table(meta, top, half_ref[0], which, capacity, slots)
        weight = jnp.zeros(held.shape, F32)
        for k in range(top):
            weight = weight + jnp.where(match[k], meta[:, top + k : top + k + 1], 0.0)
        picks.append(held)
        weighted.append(held * weight)
    pick = jnp.concatenate(picks, 0).astype(BF16)
    rows = jnp.concatenate([own_ref[:, : 2 * width], far_ref[:, : 2 * width]], 0)
    out_ref[:, : 2 * width] = dot(pick, rows, 0, 0).astype(BF16)
    ones = jnp.ones((pick.shape[0], LANES), BF16)
    weights = jnp.concatenate(weighted, 0).astype(BF16)
    out_ref[:, 2 * width :] = dot(weights, ones, 0, 0).astype(BF16)


def expert_kernel(parts, *refs):
    got = refs[:parts]
    wgu_ref, wd_ref = refs[parts : parts + 2]
    dx_out = refs[parts + 2 : 2 * parts + 2]
    gg_ref, gu_ref, act_ref = refs[2 * parts + 2 :]
    width = wd_ref.shape[2]
    slots = got[0].shape[0]
    xs = jnp.concatenate([r[:, :width] for r in got], 0)
    dys = jnp.concatenate([r[:, width : 2 * width] for r in got], 0)
    weight = jnp.concatenate([r[:, 2 * width :] for r in got], 0).astype(F32)[:, 0:1]
    gate = dot(xs, wgu_ref[0, 0], 1, 1)
    upper = dot(xs, wgu_ref[0, 1], 1, 1)
    err = dot(dys, wd_ref[0], 1, 1)
    sig = jax.nn.sigmoid(gate)
    silu = gate * sig
    act = silu * upper
    score = jnp.sum(err * act, axis=1, keepdims=True)
    delta = weight * err
    gg = (delta * upper * sig * (1.0 + gate * (1.0 - sig))).astype(BF16)
    gu = (delta * silu).astype(BF16)
    gg_ref[...] = gg
    gu_ref[...] = gu
    act_ref[...] = act.astype(BF16)
    score_col = jnp.broadcast_to(score, (score.shape[0], LANES)).astype(BF16)
    dx = (dot(gg, wgu_ref[0, 0], 1, 0) + dot(gu, wgu_ref[0, 1], 1, 0)).astype(BF16)
    for i in range(parts):
        dx_out[i][:, :width] = dx[i * slots : (i + 1) * slots]
        dx_out[i][:, width:] = score_col[i * slots : (i + 1) * slots]


def weights_kernel(parts, *refs):
    got = refs[:parts]
    gg_ref, gu_ref, act_ref, dgu_hbm, dd_hbm, buf, sems = refs[parts:]
    width = buf.shape[2]
    copies = [
        pltpu.make_async_copy(buf.at[0], dgu_hbm.at[0, 0], sems.at[0]),
        pltpu.make_async_copy(buf.at[1], dgu_hbm.at[0, 1], sems.at[1]),
        pltpu.make_async_copy(buf.at[2], dd_hbm.at[0], sems.at[2]),
    ]
    xs = jnp.concatenate([r[:, :width] for r in got], 0)
    buf[0] = dot(gg_ref[...], xs, 0, 0).astype(BF16)
    copies[0].start()
    buf[1] = dot(gu_ref[...], xs, 0, 0).astype(BF16)
    copies[1].start()
    scaled = jnp.concatenate(
        [
            (r[:, 2 * width : 2 * width + 1].astype(F32) * r[:, width : 2 * width].astype(F32)).astype(BF16)
            for r in got
        ],
        0,
    )
    buf[2] = dot(act_ref[...], scaled, 0, 0).astype(BF16)
    copies[2].start()
    for c in copies:
        c.wait()


def add_kernel(parts, *refs):
    total = refs[0][...].astype(F32)
    for r in refs[1:parts]:
        total = total + r[...].astype(F32)
    refs[parts][...] = total.astype(BF16)


def combine_kernel(top, capacity, half_ref, back_ref, own_ref, far_ref, own_out, far_out):
    slots, width = back_ref.shape[0], back_ref.shape[1] - LANES
    lane = lax.broadcasted_iota(jnp.int32, (own_ref.shape[0], LANES), 1)
    for which, (meta_ref, out_ref) in enumerate(((own_ref, own_out), (far_ref, far_out))):
        meta = meta_ref[:, 2 * width :].astype(F32)
        match, held = slot_table(meta, top, half_ref[0], which, capacity, slots)
        dx = dot(held.astype(BF16), back_ref[:, :width], 1, 0)
        probs = jnp.zeros(lane.shape, F32)
        for k in range(top):
            one = jnp.where(match[k], held, 0.0).astype(BF16)
            probs = jnp.where(lane == k, dot(one, back_ref[:, width:], 1, 0), probs)
        out_ref[:, :width] = dx.astype(out_ref.dtype)
        out_ref[:, width:] = probs.astype(out_ref.dtype)


def final_kernel(own_ref, far_ref, dx_ref, dp_ref):
    width, top = dx_ref.shape[1], dp_ref.shape[0]
    dx_ref[...] = (own_ref[:, :width] + far_ref[:, :width].astype(F32)).astype(BF16)
    probs = (own_ref[:, width:] + far_ref[:, width:].astype(F32)).astype(BF16)
    dp_ref[...] = dot(lane_map(top, 0), probs, 1, 1)


def params(mib):
    return pltpu.CompilerParams(vmem_limit_bytes=mib * 1024 * 1024)


VMEM = pl.BlockSpec(memory_space=pltpu.VMEM)
SMEM = pl.BlockSpec(memory_space=pltpu.SMEM)
ANY = pl.BlockSpec(memory_space=pl.ANY)


def body(tokens, out_grads, route_ids, route_probs, w_gate_up, w_down):
    rows, width = tokens.shape
    top = route_ids.shape[1]
    groups, parts = lax.axis_size("seq"), lax.axis_size("slice")
    experts = groups * 4
    hidden = w_down.shape[1]
    capacity = max(2, (rows * top * 4 // 3 + experts - 1) // experts)
    devices = groups * 2
    slots = devices * 2 * capacity
    total = slots * parts
    sd = jax.ShapeDtypeStruct

    def within_half(v):
        return lax.all_to_all(
            v.reshape(devices, 2 * capacity, v.shape[1]),
            ("seq", "zl"),
            split_axis=0,
            concat_axis=0,
            tiled=True,
        ).reshape(v.shape)

    def mirror(v):
        return lax.ppermute(v, ("zh", "zl"), [(i, 3 - i) for i in range(4)])

    def across(v, step):
        return lax.ppermute(v, "slice", [(i, (i + step) % parts) for i in range(parts)])

    half = lax.axis_index("zh").astype(jnp.int32).reshape(1)
    own = pl.pallas_call(
        pack_kernel,
        out_shape=sd((rows, 2 * width + LANES), BF16),
        in_specs=[ANY, ANY, VMEM, VMEM],
        out_specs=VMEM,
        scratch_shapes=[pltpu.SemaphoreType.DMA((2,))],
        compiler_params=params(4),
        name="pack",
    )(tokens, out_grads, route_ids.T, route_probs.T)
    far = mirror(own)
    picked = pl.pallas_call(
        lambda *r: select_kernel(top, capacity, *r),
        out_shape=sd((slots, 2 * width + LANES), BF16),
        in_specs=[SMEM, VMEM, VMEM],
        out_specs=VMEM,
        compiler_params=params(8),
        name="select",
    )(half, own, far)
    mine = within_half(picked)
    got = [mine] + [across(mine, i) for i in range(1, parts)]

    big = params(30)
    outs = pl.pallas_call(
        lambda *r: expert_kernel(parts, *r),
        out_shape=[sd((slots, width + LANES), BF16)] * parts + [sd((total, hidden), BF16)] * 3,
        in_specs=[VMEM] * (parts + 2),
        out_specs=[VMEM] * (parts + 3),
        compiler_params=big,
        name="expert",
    )(*got, w_gate_up, w_down)
    dx_parts, (gg, gu, act) = outs[:parts], outs[parts:]
    returned = [dx_parts[0]] + [across(dx_parts[i], -i) for i in range(1, parts)]
    summed = pl.pallas_call(
        lambda *r: add_kernel(parts, *r),
        out_shape=sd((slots, width + LANES), BF16),
        in_specs=[VMEM] * parts,
        out_specs=VMEM,
        compiler_params=params(12),
        name="add",
    )(*returned)
    back = within_half(summed)
    grad_gu, grad_down = pl.pallas_call(
        lambda *r: weights_kernel(parts, *r),
        out_shape=[sd(w_gate_up.shape, BF16), sd(w_down.shape, BF16)],
        in_specs=[VMEM] * (parts + 3),
        out_specs=[ANY] * 2,
        scratch_shapes=[
            pltpu.VMEM((3, hidden, width), BF16),
            pltpu.SemaphoreType.DMA((3,)),
        ],
        compiler_params=params(40),
        cost_estimate=pl.CostEstimate(
            flops=6 * hidden * total * width,
            bytes_accessed=10 * hidden * width,
            transcendentals=0,
        ),
        name="weights",
    )(*got, gg, gu, act)
    own_sum, far_sum = pl.pallas_call(
        lambda *r: combine_kernel(top, capacity, *r),
        out_shape=[sd((rows, width + LANES), F32), sd((rows, width + LANES), BF16)],
        in_specs=[SMEM] + [VMEM] * 3,
        out_specs=[VMEM] * 2,
        compiler_params=params(8),
        name="combine",
    )(half, back, own, far)
    home = mirror(far_sum)
    grad_tokens, grad_probs = pl.pallas_call(
        final_kernel,
        out_shape=[sd((rows, width), BF16), sd((top, rows), F32)],
        in_specs=[VMEM] * 2,
        out_specs=[VMEM] * 2,
        compiler_params=params(4),
        name="final",
    )(own_sum, home)
    return grad_tokens, grad_probs.T, grad_gu, grad_down


def solution(mesh):
    groups, columns = mesh.devices.shape
    every = ("seq", "zh", "zl", "slice")
    split = Mesh(mesh.devices.reshape(groups, 2, 2, columns // 4), every)

    def spec(rank):
        return P(every, *([None] * (rank - 1)))

    return jax.shard_map(
        body,
        mesh=split,
        in_specs=(spec(2), spec(2), spec(2), spec(2), spec(4), spec(3)),
        out_specs=(spec(2), spec(2), spec(4), spec(3)),
        check_vma=False,
    )
```

```python
import jax
import jax.numpy as jnp
from jax import lax
from jax.experimental import pallas as pl
from jax.experimental.pallas import tpu as pltpu
from jax.sharding import Mesh
from jax.sharding import PartitionSpec as P

LANES = 128
F32, BF16 = jnp.float32, jnp.bfloat16


def dot(a, b, ca, cb):
    return lax.dot_general(a, b, (((ca,), (cb,)), ((), ())), preferred_element_type=F32)


def lane_map(count, start):
    row = lax.broadcasted_iota(jnp.int32, (count, LANES), 0)
    lane = lax.broadcasted_iota(jnp.int32, (count, LANES), 1)
    return (lane == row + start).astype(BF16)


def slot_table(meta, top, upper_half, which, capacity, slots):
    rows = meta.shape[0]
    lane = lax.broadcasted_iota(jnp.int32, (rows, slots), 1)
    device = lane // (2 * capacity)
    expert = ((device // 2) * 4 + upper_half * 2 + device % 2).astype(F32)
    mine = (lane // capacity) % 2 == which
    place = (lane % capacity).astype(F32)
    match = [meta[:, k : k + 1] == expert for k in range(top)]
    named = jnp.zeros((rows, slots), F32)
    for m in match:
        named = named + m.astype(F32)
    earlier = lax.broadcasted_iota(jnp.int32, (rows, rows), 1) < lax.broadcasted_iota(
        jnp.int32, (rows, rows), 0
    )
    rank = dot(earlier.astype(BF16), named.astype(BF16), 1, 0)
    held = jnp.where(mine & (rank == place), named, 0.0)
    return match, held


def pack_kernel(x_hbm, dy_hbm, ids_hbm, p_hbm, out_ref, ids_ref, p_ref, sems):
    width, top = x_hbm.shape[1], ids_ref.shape[0]
    small = [
        pltpu.make_async_copy(ids_hbm, ids_ref, sems.at[2]),
        pltpu.make_async_copy(p_hbm, p_ref, sems.at[3]),
    ]
    copies = [
        pltpu.make_async_copy(x_hbm, out_ref.at[:, pl.ds(0, width)], sems.at[0]),
        pltpu.make_async_copy(dy_hbm, out_ref.at[:, pl.ds(width, width)], sems.at[1]),
    ]
    for c in small + copies:
        c.start()
    for c in small:
        c.wait()
    ids = ids_ref[...].astype(F32).astype(BF16)
    meta = dot(ids, lane_map(top, 0), 0, 0) + dot(p_ref[...], lane_map(top, top), 0, 0)
    out_ref[:, 2 * width :] = meta.astype(BF16)
    for c in copies:
        c.wait()


def stage_kernel(src_hbm, out_ref, sem):
    copy = pltpu.make_async_copy(src_hbm, out_ref, sem)
    copy.start()
    copy.wait()


def select_kernel(top, capacity, half_ref, own_ref, far_ref, out_ref):
    slots, width = out_ref.shape[0], (out_ref.shape[1] - LANES) // 2
    picks, weighted = [], []
    for which, ref in enumerate((own_ref, far_ref)):
        meta = ref[:, 2 * width :].astype(F32)
        match, held = slot_table(meta, top, half_ref[0], which, capacity, slots)
        weight = jnp.zeros(held.shape, F32)
        for k in range(top):
            weight = weight + jnp.where(match[k], meta[:, top + k : top + k + 1], 0.0)
        picks.append(held)
        weighted.append(held * weight)
    pick = jnp.concatenate(picks, 0).astype(BF16)
    rows = jnp.concatenate([own_ref[:, : 2 * width], far_ref[:, : 2 * width]], 0)
    out_ref[:, : 2 * width] = dot(pick, rows, 0, 0).astype(BF16)
    ones = jnp.ones((pick.shape[0], LANES), BF16)
    weights = jnp.concatenate(weighted, 0).astype(BF16)
    out_ref[:, 2 * width :] = dot(weights, ones, 0, 0).astype(BF16)


def expert_kernel(parts, *refs):
    got = refs[:parts]
    wgu_ref, wd_ref = refs[parts : parts + 2]
    dx_out = refs[parts + 2 : 2 * parts + 2]
    gg_ref, gu_ref, act_ref = refs[2 * parts + 2 :]
    width = wd_ref.shape[2]
    slots = got[0].shape[0]
    xs = jnp.concatenate([r[:, :width] for r in got], 0)
    dys = jnp.concatenate([r[:, width : 2 * width] for r in got], 0)
    weight = jnp.concatenate([r[:, 2 * width :] for r in got], 0).astype(F32)[:, 0:1]
    gate = dot(xs, wgu_ref[0, 0], 1, 1)
    upper = dot(xs, wgu_ref[0, 1], 1, 1)
    err = dot(dys, wd_ref[0], 1, 1)
    sig = jax.nn.sigmoid(gate)
    silu = gate * sig
    act = silu * upper
    score = jnp.sum(err * act, axis=1, keepdims=True)
    delta = weight * err
    gg = (delta * upper * sig * (1.0 + gate * (1.0 - sig))).astype(BF16)
    gu = (delta * silu).astype(BF16)
    gg_ref[...] = gg
    gu_ref[...] = gu
    act_ref[...] = act.astype(BF16)
    score_col = jnp.broadcast_to(score, (score.shape[0], LANES)).astype(BF16)
    dx = (dot(gg, wgu_ref[0, 0], 1, 0) + dot(gu, wgu_ref[0, 1], 1, 0)).astype(BF16)
    for i in range(parts):
        dx_out[i][:, :width] = dx[i * slots : (i + 1) * slots]
        dx_out[i][:, width:] = score_col[i * slots : (i + 1) * slots]


def weights_kernel(parts, *refs):
    got = refs[:parts]
    gg_ref, gu_ref, act_ref, dgu_hbm, dd_hbm, buf, sems = refs[parts:]
    width = buf.shape[2]
    copies = [
        pltpu.make_async_copy(buf.at[0], dgu_hbm.at[0, 0], sems.at[0]),
        pltpu.make_async_copy(buf.at[1], dgu_hbm.at[0, 1], sems.at[1]),
        pltpu.make_async_copy(buf.at[2], dd_hbm.at[0], sems.at[2]),
    ]
    xs = jnp.concatenate([r[:, :width] for r in got], 0)
    buf[0] = dot(gg_ref[...], xs, 0, 0).astype(BF16)
    copies[0].start()
    buf[1] = dot(gu_ref[...], xs, 0, 0).astype(BF16)
    copies[1].start()
    scaled = jnp.concatenate(
        [
            (r[:, 2 * width : 2 * width + 1].astype(F32) * r[:, width : 2 * width].astype(F32)).astype(BF16)
            for r in got
        ],
        0,
    )
    buf[2] = dot(act_ref[...], scaled, 0, 0).astype(BF16)
    copies[2].start()
    for c in copies:
        c.wait()


def add_kernel(parts, *refs):
    total = refs[0][...].astype(F32)
    for r in refs[1:parts]:
        total = total + r[...].astype(F32)
    refs[parts][...] = total.astype(BF16)


def combine_kernel(top, capacity, half_ref, back_ref, own_ref, far_ref, own_out, far_out):
    slots, width = back_ref.shape[0], back_ref.shape[1] - LANES
    lane = lax.broadcasted_iota(jnp.int32, (own_ref.shape[0], LANES), 1)
    for which, (meta_ref, out_ref) in enumerate(((own_ref, own_out), (far_ref, far_out))):
        meta = meta_ref[:, 2 * width :].astype(F32)
        match, held = slot_table(meta, top, half_ref[0], which, capacity, slots)
        dx = dot(held.astype(BF16), back_ref[:, :width], 1, 0)
        probs = jnp.zeros(lane.shape, F32)
        for k in range(top):
            one = jnp.where(match[k], held, 0.0).astype(BF16)
            probs = jnp.where(lane == k, dot(one, back_ref[:, width:], 1, 0), probs)
        out_ref[:, :width] = dx.astype(out_ref.dtype)
        out_ref[:, width:] = probs.astype(out_ref.dtype)


def final_kernel(own_ref, far_ref, dx_ref, dp_ref):
    width, top = dx_ref.shape[1], dp_ref.shape[0]
    dx_ref[...] = (own_ref[:, :width] + far_ref[:, :width].astype(F32)).astype(BF16)
    probs = (own_ref[:, width:] + far_ref[:, width:].astype(F32)).astype(BF16)
    dp_ref[...] = dot(lane_map(top, 0), probs, 1, 1)


def params(mib):
    return pltpu.CompilerParams(vmem_limit_bytes=mib * 1024 * 1024)


VMEM = pl.BlockSpec(memory_space=pltpu.VMEM)
SMEM = pl.BlockSpec(memory_space=pltpu.SMEM)
ANY = pl.BlockSpec(memory_space=pl.ANY)
HBM = pl.BlockSpec(memory_space=pltpu.HBM)


def body(tokens, out_grads, route_ids, route_probs, w_gate_up, w_down):
    rows, width = tokens.shape
    top = route_ids.shape[1]
    groups, parts = lax.axis_size("seq"), lax.axis_size("slice")
    experts = groups * 4
    hidden = w_down.shape[1]
    capacity = max(2, (rows * top * 4 // 3 + experts - 1) // experts)
    devices = groups * 2
    slots = devices * 2 * capacity
    total = slots * parts
    sd = jax.ShapeDtypeStruct

    def within_half(v):
        return lax.all_to_all(
            v.reshape(devices, 2 * capacity, v.shape[1]),
            ("seq", "zl"),
            split_axis=0,
            concat_axis=0,
            tiled=True,
        ).reshape(v.shape)

    def mirror(v):
        return lax.ppermute(v, ("zh", "zl"), [(i, 3 - i) for i in range(4)])

    def across(v, step):
        return lax.ppermute(v, "slice", [(i, (i + step) % parts) for i in range(parts)])

    half = lax.axis_index("zh").astype(jnp.int32).reshape(1)
    own = pl.pallas_call(
        pack_kernel,
        out_shape=sd((rows, 2 * width + LANES), BF16),
        in_specs=[HBM] * 4,
        out_specs=VMEM,
        scratch_shapes=[
            pltpu.VMEM((top, rows), jnp.int32),
            pltpu.VMEM((top, rows), BF16),
            pltpu.SemaphoreType.DMA((4,)),
        ],
        compiler_params=params(60),
        name="pack",
    )(tokens, out_grads, route_ids.T, route_probs.T)
    far = mirror(own)
    staged = pl.pallas_call(
        stage_kernel,
        out_shape=sd(w_gate_up.shape, BF16),
        in_specs=[HBM],
        out_specs=VMEM,
        scratch_shapes=[pltpu.SemaphoreType.DMA],
        compiler_params=params(44),
        cost_estimate=pl.CostEstimate(flops=0, bytes_accessed=8 * hidden * width, transcendentals=0),
        name="stage",
    )(w_gate_up)
    far, staged = lax.optimization_barrier((far, staged))
    picked = pl.pallas_call(
        lambda *r: select_kernel(top, capacity, *r),
        out_shape=sd((slots, 2 * width + LANES), BF16),
        in_specs=[SMEM, VMEM, VMEM],
        out_specs=VMEM,
        compiler_params=params(8),
        name="select",
    )(half, own, far)
    mine = within_half(picked)
    got = [mine] + [across(mine, i) for i in range(1, parts)]

    big = params(30)
    outs = pl.pallas_call(
        lambda *r: expert_kernel(parts, *r),
        out_shape=[sd((slots, width + LANES), BF16)] * parts + [sd((total, hidden), BF16)] * 3,
        in_specs=[VMEM] * (parts + 2),
        out_specs=[VMEM] * (parts + 3),
        compiler_params=big,
        name="expert",
    )(*got, staged, w_down)
    dx_parts, (gg, gu, act) = outs[:parts], outs[parts:]
    returned = [dx_parts[0]] + [across(dx_parts[i], -i) for i in range(1, parts)]
    summed = pl.pallas_call(
        lambda *r: add_kernel(parts, *r),
        out_shape=sd((slots, width + LANES), BF16),
        in_specs=[VMEM] * parts,
        out_specs=VMEM,
        compiler_params=params(12),
        name="add",
    )(*returned)
    back = within_half(summed)
    grad_gu, grad_down = pl.pallas_call(
        lambda *r: weights_kernel(parts, *r),
        out_shape=[sd(w_gate_up.shape, BF16), sd(w_down.shape, BF16)],
        in_specs=[VMEM] * (parts + 3),
        out_specs=[ANY] * 2,
        scratch_shapes=[
            pltpu.VMEM((3, hidden, width), BF16),
            pltpu.SemaphoreType.DMA((3,)),
        ],
        compiler_params=params(40),
        cost_estimate=pl.CostEstimate(
            flops=6 * hidden * total * width,
            bytes_accessed=10 * hidden * width,
            transcendentals=0,
        ),
        name="weights",
    )(*got, gg, gu, act)
    own_sum, far_sum = pl.pallas_call(
        lambda *r: combine_kernel(top, capacity, *r),
        out_shape=[sd((rows, width + LANES), F32), sd((rows, width + LANES), BF16)],
        in_specs=[SMEM] + [VMEM] * 3,
        out_specs=[VMEM] * 2,
        compiler_params=params(8),
        name="combine",
    )(half, back, own, far)
    home = mirror(far_sum)
    grad_tokens, grad_probs = pl.pallas_call(
        final_kernel,
        out_shape=[sd((rows, width), BF16), sd((top, rows), F32)],
        in_specs=[VMEM] * 2,
        out_specs=[VMEM] * 2,
        compiler_params=params(4),
        name="final",
    )(own_sum, home)
    return grad_tokens, grad_probs.T, grad_gu, grad_down


def solution(mesh):
    groups, columns = mesh.devices.shape
    every = ("seq", "zh", "zl", "slice")
    split = Mesh(mesh.devices.reshape(groups, 2, 2, columns // 4), every)

    def spec(rank):
        return P(every, *([None] * (rank - 1)))

    return jax.shard_map(
        body,
        mesh=split,
        in_specs=(spec(2), spec(2), spec(2), spec(2), spec(4), spec(3)),
        out_specs=(spec(2), spec(2), spec(4), spec(3)),
        check_vma=False,
    )
```

```python
import jax
import jax.numpy as jnp
from jax import lax
from jax.experimental import pallas as pl
from jax.experimental.pallas import tpu as pltpu
from jax.sharding import Mesh
from jax.sharding import PartitionSpec as P

LANES = 128
F32, BF16 = jnp.float32, jnp.bfloat16


def dot(a, b, ca, cb):
    return lax.dot_general(a, b, (((ca,), (cb,)), ((), ())), preferred_element_type=F32)


def lane_map(count, start):
    row = lax.broadcasted_iota(jnp.int32, (count, LANES), 0)
    lane = lax.broadcasted_iota(jnp.int32, (count, LANES), 1)
    return (lane == row + start).astype(BF16)


def slot_table(meta, top, upper_half, which, capacity, slots):
    rows = meta.shape[0]
    lane = lax.broadcasted_iota(jnp.int32, (rows, slots), 1)
    device = lane // (2 * capacity)
    expert = ((device // 2) * 4 + upper_half * 2 + device % 2).astype(F32)
    mine = (lane // capacity) % 2 == which
    place = (lane % capacity).astype(F32)
    match = [meta[:, k : k + 1] == expert for k in range(top)]
    named = jnp.zeros((rows, slots), F32)
    for m in match:
        named = named + m.astype(F32)
    earlier = lax.broadcasted_iota(jnp.int32, (rows, rows), 1) < lax.broadcasted_iota(
        jnp.int32, (rows, rows), 0
    )
    rank = dot(earlier.astype(BF16), named.astype(BF16), 1, 0)
    held = jnp.where(mine & (rank == place), named, 0.0)
    return match, held


def pack_kernel(x_hbm, dy_hbm, ids_hbm, p_hbm, out_ref, ids_ref, p_ref, sems):
    width, top = x_hbm.shape[1], ids_ref.shape[0]
    small = [
        pltpu.make_async_copy(ids_hbm, ids_ref, sems.at[2]),
        pltpu.make_async_copy(p_hbm, p_ref, sems.at[3]),
    ]
    copies = [
        pltpu.make_async_copy(x_hbm, out_ref.at[:, pl.ds(0, width)], sems.at[0]),
        pltpu.make_async_copy(dy_hbm, out_ref.at[:, pl.ds(width, width)], sems.at[1]),
    ]
    for c in small + copies:
        c.start()
    for c in small:
        c.wait()
    ids = ids_ref[...].astype(F32).astype(BF16)
    meta = dot(ids, lane_map(top, 0), 0, 0) + dot(p_ref[...], lane_map(top, top), 0, 0)
    out_ref[:, 2 * width :] = meta.astype(BF16)
    for c in copies:
        c.wait()


def stage_kernel(src_hbm, out_ref, sem):
    copy = pltpu.make_async_copy(src_hbm, out_ref, sem)
    copy.start()
    copy.wait()


def select_kernel(top, capacity, half_ref, own_ref, far_ref, out_ref):
    slots, width = out_ref.shape[0], (out_ref.shape[1] - LANES) // 2
    picks, weighted = [], []
    for which, ref in enumerate((own_ref, far_ref)):
        meta = ref[:, 2 * width :].astype(F32)
        match, held = slot_table(meta, top, half_ref[0], which, capacity, slots)
        weight = jnp.zeros(held.shape, F32)
        for k in range(top):
            weight = weight + jnp.where(match[k], meta[:, top + k : top + k + 1], 0.0)
        picks.append(held)
        weighted.append(held * weight)
    pick = jnp.concatenate(picks, 0).astype(BF16)
    rows = jnp.concatenate([own_ref[:, : 2 * width], far_ref[:, : 2 * width]], 0)
    out_ref[:, : 2 * width] = dot(pick, rows, 0, 0).astype(BF16)
    ones = jnp.ones((pick.shape[0], LANES), BF16)
    weights = jnp.concatenate(weighted, 0).astype(BF16)
    out_ref[:, 2 * width :] = dot(weights, ones, 0, 0).astype(BF16)


def expert_kernel(parts, *refs):
    got = refs[:parts]
    wgu_ref, wd_ref = refs[parts : parts + 2]
    dx_out = refs[parts + 2 : 2 * parts + 2]
    gg_ref, gu_ref, act_ref = refs[2 * parts + 2 :]
    width = wd_ref.shape[2]
    slots = got[0].shape[0]
    xs = jnp.concatenate([r[:, :width] for r in got], 0)
    dys = jnp.concatenate([r[:, width : 2 * width] for r in got], 0)
    weight = jnp.concatenate([r[:, 2 * width :] for r in got], 0).astype(F32)[:, 0:1]
    gate = dot(xs, wgu_ref[0, 0], 1, 1)
    upper = dot(xs, wgu_ref[0, 1], 1, 1)
    err = dot(dys, wd_ref[0], 1, 1)
    sig = jax.nn.sigmoid(gate)
    silu = gate * sig
    act = silu * upper
    score = jnp.sum(err * act, axis=1, keepdims=True)
    delta = weight * err
    gg = (delta * upper * sig * (1.0 + gate * (1.0 - sig))).astype(BF16)
    gu = (delta * silu).astype(BF16)
    gg_ref[...] = gg
    gu_ref[...] = gu
    act_ref[...] = act.astype(BF16)
    score_col = jnp.broadcast_to(score, (score.shape[0], LANES)).astype(BF16)
    dx = (dot(gg, wgu_ref[0, 0], 1, 0) + dot(gu, wgu_ref[0, 1], 1, 0)).astype(BF16)
    for i in range(parts):
        dx_out[i][:, :width] = dx[i * slots : (i + 1) * slots]
        dx_out[i][:, width:] = score_col[i * slots : (i + 1) * slots]


def weights_kernel(parts, *refs):
    got = refs[:parts]
    gg_ref, gu_ref, act_ref, dgu_hbm, dd_hbm, buf, sems = refs[parts:]
    width = buf.shape[2]
    copies = [
        pltpu.make_async_copy(buf.at[0], dgu_hbm.at[0, 0], sems.at[0]),
        pltpu.make_async_copy(buf.at[1], dgu_hbm.at[0, 1], sems.at[1]),
        pltpu.make_async_copy(buf.at[2], dd_hbm.at[0], sems.at[2]),
    ]
    xs = jnp.concatenate([r[:, :width] for r in got], 0)
    buf[0] = dot(gg_ref[...], xs, 0, 0).astype(BF16)
    copies[0].start()
    buf[1] = dot(gu_ref[...], xs, 0, 0).astype(BF16)
    copies[1].start()
    scaled = jnp.concatenate(
        [
            (r[:, 2 * width : 2 * width + 1].astype(F32) * r[:, width : 2 * width].astype(F32)).astype(BF16)
            for r in got
        ],
        0,
    )
    buf[2] = dot(act_ref[...], scaled, 0, 0).astype(BF16)
    copies[2].start()
    for c in copies:
        c.wait()


def add_kernel(parts, *refs):
    total = refs[0][...].astype(F32)
    for r in refs[1:parts]:
        total = total + r[...].astype(F32)
    refs[parts][...] = total.astype(BF16)


def combine_kernel(top, capacity, half_ref, back_ref, own_ref, far_ref, own_out, far_out):
    slots, width = back_ref.shape[0], back_ref.shape[1] - LANES
    lane = lax.broadcasted_iota(jnp.int32, (own_ref.shape[0], LANES), 1)
    for which, (meta_ref, out_ref) in enumerate(((own_ref, own_out), (far_ref, far_out))):
        meta = meta_ref[:, 2 * width :].astype(F32)
        match, held = slot_table(meta, top, half_ref[0], which, capacity, slots)
        dx = dot(held.astype(BF16), back_ref[:, :width], 1, 0)
        probs = jnp.zeros(lane.shape, F32)
        for k in range(top):
            one = jnp.where(match[k], held, 0.0).astype(BF16)
            probs = jnp.where(lane == k, dot(one, back_ref[:, width:], 1, 0), probs)
        out_ref[:, :width] = dx.astype(out_ref.dtype)
        out_ref[:, width:] = probs.astype(out_ref.dtype)


def final_kernel(own_ref, far_ref, dx_ref, dp_ref):
    width, top = dx_ref.shape[1], dp_ref.shape[0]
    dx_ref[...] = (own_ref[:, :width] + far_ref[:, :width].astype(F32)).astype(BF16)
    probs = (own_ref[:, width:] + far_ref[:, width:].astype(F32)).astype(BF16)
    dp_ref[...] = dot(lane_map(top, 0), probs, 1, 1)


def in_hbm(v):
    return pltpu.with_memory_space_constraint(v, pltpu.HBM)


def params(mib):
    return pltpu.CompilerParams(vmem_limit_bytes=mib * 1024 * 1024)


VMEM = pl.BlockSpec(memory_space=pltpu.VMEM)
SMEM = pl.BlockSpec(memory_space=pltpu.SMEM)
ANY = pl.BlockSpec(memory_space=pl.ANY)
HBM = pl.BlockSpec(memory_space=pltpu.HBM)


def body(tokens, out_grads, route_ids, route_probs, w_gate_up, w_down):
    rows, width = tokens.shape
    top = route_ids.shape[1]
    groups, parts = lax.axis_size("seq"), lax.axis_size("slice")
    experts = groups * 4
    hidden = w_down.shape[1]
    capacity = max(2, (rows * top * 4 // 3 + experts - 1) // experts)
    devices = groups * 2
    slots = devices * 2 * capacity
    total = slots * parts
    sd = jax.ShapeDtypeStruct

    def within_half(v):
        return lax.all_to_all(
            v.reshape(devices, 2 * capacity, v.shape[1]),
            ("seq", "zl"),
            split_axis=0,
            concat_axis=0,
            tiled=True,
        ).reshape(v.shape)

    def mirror(v):
        return lax.ppermute(v, ("zh", "zl"), [(i, 3 - i) for i in range(4)])

    def across(v, step):
        return lax.ppermute(v, "slice", [(i, (i + step) % parts) for i in range(parts)])

    half = lax.axis_index("zh").astype(jnp.int32).reshape(1)
    own = pl.pallas_call(
        pack_kernel,
        out_shape=pltpu.VMEM((rows, 2 * width + LANES), BF16),
        in_specs=[HBM] * 4,
        out_specs=VMEM,
        scratch_shapes=[
            pltpu.VMEM((top, rows), jnp.int32),
            pltpu.VMEM((top, rows), BF16),
            pltpu.SemaphoreType.DMA((4,)),
        ],
        compiler_params=params(4),
        name="pack",
    )(*[in_hbm(v) for v in (tokens, out_grads, route_ids.T, route_probs.T)])
    far = mirror(own)
    staged = pl.pallas_call(
        stage_kernel,
        out_shape=pltpu.VMEM(w_gate_up.shape, BF16),
        in_specs=[HBM],
        out_specs=VMEM,
        scratch_shapes=[pltpu.SemaphoreType.DMA],
        compiler_params=params(4),
        cost_estimate=pl.CostEstimate(flops=0, bytes_accessed=8 * hidden * width, transcendentals=0),
        name="stage",
    )(in_hbm(w_gate_up))
    far, staged = lax.optimization_barrier((far, staged))
    picked = pl.pallas_call(
        lambda *r: select_kernel(top, capacity, *r),
        out_shape=sd((slots, 2 * width + LANES), BF16),
        in_specs=[SMEM, VMEM, VMEM],
        out_specs=VMEM,
        compiler_params=params(8),
        name="select",
    )(half, own, far)
    mine = within_half(picked)
    got = [mine] + [across(mine, i) for i in range(1, parts)]

    big = params(30)
    outs = pl.pallas_call(
        lambda *r: expert_kernel(parts, *r),
        out_shape=[sd((slots, width + LANES), BF16)] * parts + [sd((total, hidden), BF16)] * 3,
        in_specs=[VMEM] * (parts + 2),
        out_specs=[VMEM] * (parts + 3),
        compiler_params=big,
        name="expert",
    )(*got, staged, w_down)
    dx_parts, (gg, gu, act) = outs[:parts], outs[parts:]
    returned = [dx_parts[0]] + [across(dx_parts[i], -i) for i in range(1, parts)]
    summed = pl.pallas_call(
        lambda *r: add_kernel(parts, *r),
        out_shape=sd((slots, width + LANES), BF16),
        in_specs=[VMEM] * parts,
        out_specs=VMEM,
        compiler_params=params(12),
        name="add",
    )(*returned)
    back = within_half(summed)
    grad_gu, grad_down = pl.pallas_call(
        lambda *r: weights_kernel(parts, *r),
        out_shape=[sd(w_gate_up.shape, BF16), sd(w_down.shape, BF16)],
        in_specs=[VMEM] * (parts + 3),
        out_specs=[ANY] * 2,
        scratch_shapes=[
            pltpu.VMEM((3, hidden, width), BF16),
            pltpu.SemaphoreType.DMA((3,)),
        ],
        compiler_params=params(40),
        cost_estimate=pl.CostEstimate(
            flops=6 * hidden * total * width,
            bytes_accessed=10 * hidden * width,
            transcendentals=0,
        ),
        name="weights",
    )(*got, gg, gu, act)
    own_sum, far_sum = pl.pallas_call(
        lambda *r: combine_kernel(top, capacity, *r),
        out_shape=[sd((rows, width + LANES), F32), sd((rows, width + LANES), BF16)],
        in_specs=[SMEM] + [VMEM] * 3,
        out_specs=[VMEM] * 2,
        compiler_params=params(8),
        name="combine",
    )(half, back, own, far)
    home = mirror(far_sum)
    grad_tokens, grad_probs = pl.pallas_call(
        final_kernel,
        out_shape=[sd((rows, width), BF16), sd((top, rows), F32)],
        in_specs=[VMEM] * 2,
        out_specs=[VMEM] * 2,
        compiler_params=params(4),
        name="final",
    )(own_sum, home)
    return grad_tokens, grad_probs.T, grad_gu, grad_down


def solution(mesh):
    groups, columns = mesh.devices.shape
    every = ("seq", "zh", "zl", "slice")
    split = Mesh(mesh.devices.reshape(groups, 2, 2, columns // 4), every)

    def spec(rank):
        return P(every, *([None] * (rank - 1)))

    return jax.shard_map(
        body,
        mesh=split,
        in_specs=(spec(2), spec(2), spec(2), spec(2), spec(4), spec(3)),
        out_specs=(spec(2), spec(2), spec(4), spec(3)),
        check_vma=False,
    )
```

```python
import jax
import jax.numpy as jnp
from jax import lax
from jax.experimental import pallas as pl
from jax.experimental.pallas import tpu as pltpu
from jax.sharding import Mesh
from jax.sharding import PartitionSpec as P

LANES = 128
F32, BF16 = jnp.float32, jnp.bfloat16


def dot(a, b, ca, cb):
    return lax.dot_general(a, b, (((ca,), (cb,)), ((), ())), preferred_element_type=F32)


def lane_map(count, start):
    row = lax.broadcasted_iota(jnp.int32, (count, LANES), 0)
    lane = lax.broadcasted_iota(jnp.int32, (count, LANES), 1)
    return (lane == row + start).astype(BF16)


def slot_table(meta, top, upper_half, which, capacity, slots):
    rows = meta.shape[0]
    lane = lax.broadcasted_iota(jnp.int32, (rows, slots), 1)
    device = lane // (2 * capacity)
    expert = ((device // 2) * 4 + upper_half * 2 + device % 2).astype(F32)
    mine = (lane // capacity) % 2 == which
    place = (lane % capacity).astype(F32)
    match = [meta[:, k : k + 1] == expert for k in range(top)]
    named = jnp.zeros((rows, slots), F32)
    for m in match:
        named = named + m.astype(F32)
    earlier = lax.broadcasted_iota(jnp.int32, (rows, rows), 1) < lax.broadcasted_iota(
        jnp.int32, (rows, rows), 0
    )
    rank = dot(earlier.astype(BF16), named.astype(BF16), 1, 0)
    held = jnp.where(mine & (rank == place), named, 0.0)
    return match, held


def pack_kernel(x_hbm, dy_hbm, ids_hbm, out_ref, ids_ref, sems):
    width, top = x_hbm.shape[1], ids_ref.shape[0]
    copies = [
        pltpu.make_async_copy(ids_hbm, ids_ref, sems.at[2]),
        pltpu.make_async_copy(x_hbm, out_ref.at[:, pl.ds(0, width)], sems.at[0]),
        pltpu.make_async_copy(dy_hbm, out_ref.at[:, pl.ds(width, width)], sems.at[1]),
    ]
    for c in copies:
        c.start()
    copies[0].wait()
    ids = ids_ref[...].astype(F32).astype(BF16)
    out_ref[:, 2 * width :] = dot(ids, lane_map(top, 0), 0, 0).astype(BF16)
    for c in copies[1:]:
        c.wait()


def stage_kernel(src_hbm, out_ref, sem):
    copy = pltpu.make_async_copy(src_hbm, out_ref, sem)
    copy.start()
    copy.wait()


def select_kernel(capacity, half_ref, own_ref, far_ref, own_p_ref, far_p_ref, out_ref):
    slots, width, top = out_ref.shape[0], out_ref.shape[1] // 2, own_p_ref.shape[0]
    picks, weighted = [], []
    for which, (ref, p_ref) in enumerate(((own_ref, own_p_ref), (far_ref, far_p_ref))):
        probs = dot(p_ref[...], lane_map(top, 0), 0, 0)
        meta = ref[:, 2 * width :].astype(F32)
        match, held = slot_table(meta, top, half_ref[0], which, capacity, slots)
        weight = jnp.zeros(held.shape, F32)
        for k in range(top):
            weight = weight + jnp.where(match[k], probs[:, k : k + 1], 0.0)
        picks.append(held)
        weighted.append(held * weight)
    for i, mask in enumerate((picks, weighted)):
        cut = slice(i * width, (i + 1) * width)
        rows = jnp.concatenate([own_ref[:, cut], far_ref[:, cut]], 0)
        out_ref[:, cut] = dot(jnp.concatenate(mask, 0).astype(BF16), rows, 0, 0).astype(BF16)


def expert_kernel(parts, *refs):
    got = refs[:parts]
    wgu_ref, wd_ref = refs[parts : parts + 2]
    dx_out = refs[parts + 2 : 2 * parts + 2]
    gg_ref, gu_ref, act_ref = refs[2 * parts + 2 :]
    width = wd_ref.shape[2]
    slots = got[0].shape[0]
    xs = jnp.concatenate([r[:, :width] for r in got], 0)
    dys = jnp.concatenate([r[:, width:] for r in got], 0)
    gate = dot(xs, wgu_ref[0, 0], 1, 1)
    upper = dot(xs, wgu_ref[0, 1], 1, 1)
    err = dot(dys, wd_ref[0], 1, 1)
    sig = jax.nn.sigmoid(gate)
    silu = gate * sig
    act = silu * upper
    score = jnp.sum(err * act, axis=1, keepdims=True)
    gg = (err * upper * sig * (1.0 + gate * (1.0 - sig))).astype(BF16)
    gu = (err * silu).astype(BF16)
    gg_ref[...] = gg
    gu_ref[...] = gu
    act_ref[...] = act.astype(BF16)
    score_col = jnp.broadcast_to(score, (score.shape[0], LANES)).astype(BF16)
    dx = (dot(gg, wgu_ref[0, 0], 1, 0) + dot(gu, wgu_ref[0, 1], 1, 0)).astype(BF16)
    for i in range(parts):
        dx_out[i][:, :width] = dx[i * slots : (i + 1) * slots]
        dx_out[i][:, width:] = score_col[i * slots : (i + 1) * slots]


def weights_kernel(parts, *refs):
    got = refs[:parts]
    gg_ref, gu_ref, act_ref, dgu_hbm, dd_hbm, buf, sems = refs[parts:]
    hidden, width = buf.shape[1:]
    xs = jnp.concatenate([r[:, :width] for r in got], 0)
    dys = jnp.concatenate([r[:, width:] for r in got], 0)
    outs = ((gg_ref, xs, dgu_hbm.at[0, 0]), (gu_ref, xs, dgu_hbm.at[0, 1]), (act_ref, dys, dd_hbm.at[0]))
    copies = []
    for i, (lhs_ref, rhs, out) in enumerate(outs):
        for j, start in enumerate(range(0, hidden, LANES)):
            size = min(LANES, hidden - start)
            buf[i, start : start + size, :] = dot(lhs_ref[:, start : start + size], rhs, 0, 0).astype(BF16)
            cut = pl.ds(start, size)
            copies.append(pltpu.make_async_copy(buf.at[i, cut], out.at[cut], sems.at[i, j]))
            copies[-1].start()
    for c in copies:
        c.wait()


def add_kernel(parts, *refs):
    total = refs[0][...].astype(F32)
    for r in refs[1:parts]:
        total = total + r[...].astype(F32)
    refs[parts][...] = total.astype(BF16)


def combine_kernel(top, capacity, half_ref, back_ref, own_ref, far_ref, own_out, far_out):
    slots, width = back_ref.shape[0], back_ref.shape[1] - LANES
    lane = lax.broadcasted_iota(jnp.int32, (own_ref.shape[0], LANES), 1)
    for which, (meta_ref, out_ref) in enumerate(((own_ref, own_out), (far_ref, far_out))):
        meta = meta_ref[:, 2 * width :].astype(F32)
        match, held = slot_table(meta, top, half_ref[0], which, capacity, slots)
        dx = dot(held.astype(BF16), back_ref[:, :width], 1, 0)
        probs = jnp.zeros(lane.shape, F32)
        for k in range(top):
            one = jnp.where(match[k], held, 0.0).astype(BF16)
            probs = jnp.where(lane == k, dot(one, back_ref[:, width:], 1, 0), probs)
        out_ref[:, :width] = dx.astype(out_ref.dtype)
        out_ref[:, width:] = probs.astype(out_ref.dtype)


def final_kernel(own_ref, far_ref, p_ref, dx_ref, dp_ref):
    width, top = dx_ref.shape[1], dp_ref.shape[0]
    dx_ref[...] = (own_ref[:, :width] + far_ref[:, :width].astype(F32)).astype(BF16)
    probs = (own_ref[:, width:] + far_ref[:, width:].astype(F32)).astype(BF16)
    dp_ref[...] = dot(lane_map(top, 0), probs, 1, 1) / p_ref[...].astype(F32)


def in_hbm(v):
    return pltpu.with_memory_space_constraint(v, pltpu.HBM)


def params(mib):
    return pltpu.CompilerParams(vmem_limit_bytes=mib * 1024 * 1024)


VMEM = pl.BlockSpec(memory_space=pltpu.VMEM)
SMEM = pl.BlockSpec(memory_space=pltpu.SMEM)
ANY = pl.BlockSpec(memory_space=pl.ANY)
HBM = pl.BlockSpec(memory_space=pltpu.HBM)


def body(tokens, out_grads, route_ids, route_probs, w_gate_up, w_down):
    rows, width = tokens.shape
    top = route_ids.shape[1]
    groups, parts = lax.axis_size("seq"), lax.axis_size("slice")
    experts = groups * 4
    hidden = w_down.shape[1]
    capacity = max(2, (rows * top * 4 // 3 + experts - 1) // experts)
    devices = groups * 2
    slots = devices * 2 * capacity
    total = slots * parts
    sd = jax.ShapeDtypeStruct

    def within_half(v):
        return lax.all_to_all(
            v.reshape(devices, 2 * capacity, v.shape[1]),
            ("seq", "zl"),
            split_axis=0,
            concat_axis=0,
            tiled=True,
        ).reshape(v.shape)

    def mirror(v):
        return lax.ppermute(v, ("zh", "zl"), [(i, 3 - i) for i in range(4)])

    def across(v, step):
        return lax.ppermute(v, "slice", [(i, (i + step) % parts) for i in range(parts)])

    half = lax.axis_index("zh").astype(jnp.int32).reshape(1)
    own = pl.pallas_call(
        pack_kernel,
        out_shape=pltpu.VMEM((rows, 2 * width + LANES), BF16),
        in_specs=[HBM] * 3,
        out_specs=VMEM,
        scratch_shapes=[pltpu.VMEM((top, rows), jnp.int32), pltpu.SemaphoreType.DMA((3,))],
        compiler_params=params(4),
        name="pack",
    )(*[in_hbm(v) for v in (tokens, out_grads, route_ids.T)])
    far, own_p, far_p = mirror(own), route_probs.T, mirror(route_probs).T
    staged = pl.pallas_call(
        stage_kernel,
        out_shape=pltpu.VMEM(w_gate_up.shape, BF16),
        in_specs=[HBM],
        out_specs=VMEM,
        scratch_shapes=[pltpu.SemaphoreType.DMA],
        compiler_params=params(4),
        cost_estimate=pl.CostEstimate(flops=0, bytes_accessed=8 * hidden * width, transcendentals=0),
        name="stage",
    )(in_hbm(w_gate_up))
    far, staged = lax.optimization_barrier((far, staged))
    picked = pl.pallas_call(
        lambda *r: select_kernel(capacity, *r),
        out_shape=sd((slots, 2 * width), BF16),
        in_specs=[SMEM] + [VMEM] * 4,
        out_specs=VMEM,
        compiler_params=params(8),
        name="select",
    )(half, own, far, own_p, far_p)
    mine = within_half(picked)
    got = [mine] + [across(mine, i) for i in range(1, parts)]

    big = params(30)
    outs = pl.pallas_call(
        lambda *r: expert_kernel(parts, *r),
        out_shape=[sd((slots, width + LANES), BF16)] * parts + [sd((total, hidden), BF16)] * 3,
        in_specs=[VMEM] * (parts + 2),
        out_specs=[VMEM] * (parts + 3),
        compiler_params=big,
        name="expert",
    )(*got, staged, w_down)
    dx_parts, (gg, gu, act) = outs[:parts], outs[parts:]
    returned = [dx_parts[0]] + [across(dx_parts[i], -i) for i in range(1, parts)]
    summed = pl.pallas_call(
        lambda *r: add_kernel(parts, *r),
        out_shape=sd((slots, width + LANES), BF16),
        in_specs=[VMEM] * parts,
        out_specs=VMEM,
        compiler_params=params(12),
        name="add",
    )(*returned)
    back = within_half(summed)
    grad_gu, grad_down = pl.pallas_call(
        lambda *r: weights_kernel(parts, *r),
        out_shape=[sd(w_gate_up.shape, BF16), sd(w_down.shape, BF16)],
        in_specs=[VMEM] * (parts + 3),
        out_specs=[ANY] * 2,
        scratch_shapes=[
            pltpu.VMEM((3, hidden, width), BF16),
            pltpu.SemaphoreType.DMA((3, -(-hidden // LANES))),
        ],
        compiler_params=params(40),
        cost_estimate=pl.CostEstimate(
            flops=6 * hidden * total * width,
            bytes_accessed=10 * hidden * width,
            transcendentals=0,
        ),
        name="weights",
    )(*got, gg, gu, act)
    own_sum, far_sum = pl.pallas_call(
        lambda *r: combine_kernel(top, capacity, *r),
        out_shape=[sd((rows, width + LANES), F32), sd((rows, width + LANES), BF16)],
        in_specs=[SMEM] + [VMEM] * 3,
        out_specs=[VMEM] * 2,
        compiler_params=params(8),
        name="combine",
    )(half, back, own, far)
    home = mirror(far_sum)
    grad_tokens, grad_probs = pl.pallas_call(
        final_kernel,
        out_shape=[sd((rows, width), BF16), sd((top, rows), F32)],
        in_specs=[VMEM] * 3,
        out_specs=[VMEM] * 2,
        compiler_params=params(4),
        name="final",
    )(own_sum, home, own_p)
    return grad_tokens, grad_probs.T, grad_gu, grad_down


def solution(mesh):
    groups, columns = mesh.devices.shape
    every = ("seq", "zh", "zl", "slice")
    split = Mesh(mesh.devices.reshape(groups, 2, 2, columns // 4), every)

    def spec(rank):
        return P(every, *([None] * (rank - 1)))

    return jax.shard_map(
        body,
        mesh=split,
        in_specs=(spec(2), spec(2), spec(2), spec(2), spec(4), spec(3)),
        out_specs=(spec(2), spec(2), spec(4), spec(3)),
        check_vma=False,
    )
```

```python
import jax
import jax.numpy as jnp
from jax import lax
from jax.experimental import pallas as pl
from jax.experimental.pallas import tpu as pltpu
from jax.sharding import Mesh
from jax.sharding import PartitionSpec as P

LANES = 128
F32, BF16 = jnp.float32, jnp.bfloat16


def dot(a, b, ca, cb):
    return lax.dot_general(a, b, (((ca,), (cb,)), ((), ())), preferred_element_type=F32)


def lane_map(count, start):
    row = lax.broadcasted_iota(jnp.int32, (count, LANES), 0)
    lane = lax.broadcasted_iota(jnp.int32, (count, LANES), 1)
    return (lane == row + start).astype(BF16)


def held_slots(meta, top, expert, place):
    rows = meta.shape[0]
    match = [meta[:, k : k + 1] == expert for k in range(top)]
    named = jnp.zeros(expert.shape, F32)
    for m in match:
        named = named + m.astype(F32)
    earlier = lax.broadcasted_iota(jnp.int32, (rows, rows), 1) < lax.broadcasted_iota(
        jnp.int32, (rows, rows), 0
    )
    rank = dot(earlier.astype(BF16), named.astype(BF16), 1, 0)
    return match, jnp.where(rank == place, named, 0.0)


def pack_kernel(x_hbm, dy_hbm, ids_hbm, p_hbm, out_ref, ids_ref, p_ref, sems):
    width, top = x_hbm.shape[1], ids_ref.shape[0]
    small = [
        pltpu.make_async_copy(ids_hbm, ids_ref, sems.at[2]),
        pltpu.make_async_copy(p_hbm, p_ref, sems.at[3]),
    ]
    copies = [
        pltpu.make_async_copy(x_hbm, out_ref.at[:, pl.ds(0, width)], sems.at[0]),
        pltpu.make_async_copy(dy_hbm, out_ref.at[:, pl.ds(width, width)], sems.at[1]),
    ]
    for c in small + copies:
        c.start()
    for c in small:
        c.wait()
    ids = ids_ref[...].astype(F32).astype(BF16)
    meta = dot(ids, lane_map(top, 0), 0, 0) + dot(p_ref[...], lane_map(top, top), 0, 0)
    out_ref[:, 2 * width :] = meta.astype(BF16)
    for c in copies:
        c.wait()


def stage_kernel(src_hbm, out_ref, sem):
    copy = pltpu.make_async_copy(src_hbm, out_ref, sem)
    copy.start()
    copy.wait()


def select_kernel(top, capacity, half_ref, me_ref, first_ref, second_ref, *out_refs):
    width, size = (first_ref.shape[1] - LANES) // 2, 2 * capacity
    lane = lax.broadcasted_iota(jnp.int32, (first_ref.shape[0], len(out_refs) * size), 1)
    plane = (me_ref[0] // 2) ^ (lane // size)
    expert = (plane * 4 + half_ref[0] * 2 + me_ref[0] % 2).astype(F32)
    place = (lane % capacity).astype(F32)
    picks, weighted = [], []
    for which, ref in enumerate((first_ref, second_ref)):
        meta = ref[:, 2 * width :].astype(F32)
        match, held = held_slots(meta, top, expert, place)
        held = jnp.where((lane // capacity) % 2 == which, held, 0.0)
        weight = jnp.zeros(held.shape, F32)
        for k in range(top):
            weight = weight + jnp.where(match[k], meta[:, top + k : top + k + 1], 0.0)
        picks.append(held)
        weighted.append(held * weight)
    pick = jnp.concatenate(picks, 0).astype(BF16)
    rows = jnp.concatenate([first_ref[:, : 2 * width], second_ref[:, : 2 * width]], 0)
    rows = dot(pick, rows, 0, 0).astype(BF16)
    ones = jnp.ones((pick.shape[0], LANES), BF16)
    weight = dot(jnp.concatenate(weighted, 0).astype(BF16), ones, 0, 0).astype(BF16)
    for i, out_ref in enumerate(out_refs):
        out_ref[:, : 2 * width] = rows[i * size : (i + 1) * size]
        out_ref[:, 2 * width :] = weight[i * size : (i + 1) * size]


def expert_kernel(parts, pieces, *refs):
    got = refs[:pieces]
    wgu_ref, wd_ref = refs[pieces : pieces + 2]
    dx_out = refs[pieces + 2 : pieces + 2 + parts]
    gg_ref, gu_ref, act_ref = refs[pieces + 2 + parts :]
    width, slots = wd_ref.shape[2], dx_out[0].shape[0]
    xs = jnp.concatenate([r[:, :width] for r in got], 0)
    dys = jnp.concatenate([r[:, width : 2 * width] for r in got], 0)
    weight = jnp.concatenate([r[:, 2 * width :] for r in got], 0).astype(F32)[:, 0:1]
    gate = dot(xs, wgu_ref[0, 0], 1, 1)
    upper = dot(xs, wgu_ref[0, 1], 1, 1)
    err = dot(dys, wd_ref[0], 1, 1)
    sig = jax.nn.sigmoid(gate)
    silu = gate * sig
    act = silu * upper
    score = jnp.sum(err * act, axis=1, keepdims=True)
    delta = weight * err
    gg = (delta * upper * sig * (1.0 + gate * (1.0 - sig))).astype(BF16)
    gu = (delta * silu).astype(BF16)
    gg_ref[...] = gg
    gu_ref[...] = gu
    act_ref[...] = act.astype(BF16)
    score_col = jnp.broadcast_to(score, (score.shape[0], LANES)).astype(BF16)
    dx = (dot(gg, wgu_ref[0, 0], 1, 0) + dot(gu, wgu_ref[0, 1], 1, 0)).astype(BF16)
    for i in range(parts):
        dx_out[i][:, :width] = dx[i * slots : (i + 1) * slots]
        dx_out[i][:, width:] = score_col[i * slots : (i + 1) * slots]


def weights_kernel(parts, *refs):
    got = refs[:parts]
    gg_ref, gu_ref, act_ref, dgu_hbm, dd_hbm, buf, sems = refs[parts:]
    hidden, width = buf.shape[1:]
    xs = jnp.concatenate([r[:, :width] for r in got], 0)
    weight = jnp.concatenate([r[:, 2 * width :] for r in got], 0).astype(F32)[:, 0:1]
    dys = jnp.concatenate([r[:, width : 2 * width] for r in got], 0)
    scaled = (weight * dys.astype(F32)).astype(BF16)
    outs = ((gg_ref, xs, dgu_hbm.at[0, 0]), (gu_ref, xs, dgu_hbm.at[0, 1]), (act_ref, scaled, dd_hbm.at[0]))
    copies = []
    for i, (lhs_ref, rhs, out) in enumerate(outs):
        for j, start in enumerate(range(0, hidden, LANES)):
            size = min(LANES, hidden - start)
            buf[i, start : start + size, :] = dot(lhs_ref[:, start : start + size], rhs, 0, 0).astype(BF16)
            cut = pl.ds(start, size)
            copies.append(pltpu.make_async_copy(buf.at[i, cut], out.at[cut], sems.at[i, j]))
            copies[-1].start()
    for c in copies:
        c.wait()


def add_kernel(capacity, me_ref, *refs):
    out_ref = refs[-1]
    total = refs[0][...].astype(F32)
    for r in refs[1:-1]:
        total = total + r[...].astype(F32)
    total = total.astype(BF16)
    devices = out_ref.shape[0]
    for i in range(devices):
        near, far = (total[j * capacity : (j + 1) * capacity] for j in (i, devices + i))
        out_ref[me_ref[0] ^ i] = jnp.concatenate([near, far], 0)


def combine_kernel(top, capacity, half_ref, back_ref, own_ref, far_ref, own_out, far_out):
    slots, width = back_ref.shape[0], back_ref.shape[1] - LANES
    rows = own_ref.shape[0]
    lane = lax.broadcasted_iota(jnp.int32, (rows, LANES), 1)
    slot = lax.broadcasted_iota(jnp.int32, (rows, slots), 1)
    device = slot // (2 * capacity)
    expert = ((device // 2) * 4 + half_ref[0] * 2 + device % 2).astype(F32)
    place = (slot % capacity).astype(F32)
    for which, (meta_ref, out_ref) in enumerate(((own_ref, own_out), (far_ref, far_out))):
        meta = meta_ref[:, 2 * width :].astype(F32)
        match, held = held_slots(meta, top, expert, place)
        held = jnp.where((slot // capacity) % 2 == which, held, 0.0)
        dx = dot(held.astype(BF16), back_ref[:, :width], 1, 0)
        probs = jnp.zeros(lane.shape, F32)
        for k in range(top):
            one = jnp.where(match[k], held, 0.0).astype(BF16)
            probs = jnp.where(lane == k, dot(one, back_ref[:, width:], 1, 0), probs)
        out_ref[:, :width] = dx.astype(out_ref.dtype)
        out_ref[:, width:] = probs.astype(out_ref.dtype)


def final_kernel(own_ref, far_ref, dx_ref, dp_ref):
    width, top = dx_ref.shape[1], dp_ref.shape[0]
    dx_ref[...] = (own_ref[:, :width] + far_ref[:, :width].astype(F32)).astype(BF16)
    probs = (own_ref[:, width:] + far_ref[:, width:].astype(F32)).astype(BF16)
    dp_ref[...] = dot(lane_map(top, 0), probs, 1, 1)


def in_hbm(v):
    return pltpu.with_memory_space_constraint(v, pltpu.HBM)


def params(mib):
    return pltpu.CompilerParams(vmem_limit_bytes=mib * 1024 * 1024)


VMEM = pl.BlockSpec(memory_space=pltpu.VMEM)
SMEM = pl.BlockSpec(memory_space=pltpu.SMEM)
ANY = pl.BlockSpec(memory_space=pl.ANY)
HBM = pl.BlockSpec(memory_space=pltpu.HBM)


def body(tokens, out_grads, route_ids, route_probs, w_gate_up, w_down):
    rows, width = tokens.shape
    top = route_ids.shape[1]
    groups, parts = lax.axis_size("seq"), lax.axis_size("slice")
    experts = groups * 4
    hidden = w_down.shape[1]
    capacity = max(2, (rows * top * 4 // 3 + experts - 1) // experts)
    devices = groups * 2
    slots = devices * 2 * capacity
    total = slots * parts
    sd = jax.ShapeDtypeStruct

    def within_half(v):
        return lax.all_to_all(v, ("seq", "zl"), split_axis=0, concat_axis=0, tiled=True)

    def within_plane(pieces):
        order = [d for d in reversed(range(1, groups))]
        moved = list(pieces)
        for d in order:
            moved[d] = lax.ppermute(pieces[d], "seq", [(i, i ^ d) for i in range(groups)])
        return moved

    def beside(v):
        return lax.ppermute(v, "zl", [(0, 1), (1, 0)])

    def mirror(v):
        return lax.ppermute(v, ("zh", "zl"), [(i, 3 - i) for i in range(4)])

    def across(v, step):
        return lax.ppermute(v, "slice", [(i, (i + step) % parts) for i in range(parts)])

    half = lax.axis_index("zh").astype(jnp.int32).reshape(1)
    me = lax.axis_index(("seq", "zl")).astype(jnp.int32).reshape(1)
    own = pl.pallas_call(
        pack_kernel,
        out_shape=pltpu.VMEM((rows, 2 * width + LANES), BF16),
        in_specs=[HBM] * 4,
        out_specs=VMEM,
        scratch_shapes=[
            pltpu.VMEM((top, rows), jnp.int32),
            pltpu.VMEM((top, rows), BF16),
            pltpu.SemaphoreType.DMA((4,)),
        ],
        compiler_params=params(4),
        name="pack",
    )(*[in_hbm(v) for v in (tokens, out_grads, route_ids.T, route_probs.T)])
    def select(first, second, name):
        return pl.pallas_call(
            lambda *r: select_kernel(top, capacity, *r),
            out_shape=[sd((2 * capacity, 2 * width + LANES), BF16)] * groups,
            in_specs=[SMEM, SMEM, VMEM, VMEM],
            out_specs=[VMEM] * groups,
            compiler_params=params(8),
            name=name,
        )(half, me, first, second)

    far, near = mirror(own), beside(own)
    picked = select(own, near, "near")
    relayed, _ = lax.optimization_barrier((far, picked))
    near_rows = within_plane(picked)
    beyond = beside(relayed)
    picked = select(far, beyond, "far")
    first = [across(picked[0], i) for i in range(1, parts)]
    w_held, *first = lax.optimization_barrier((w_gate_up, *first))
    staged = pl.pallas_call(
        stage_kernel,
        out_shape=pltpu.VMEM(w_gate_up.shape, BF16),
        in_specs=[HBM],
        out_specs=VMEM,
        scratch_shapes=[pltpu.SemaphoreType.DMA],
        compiler_params=params(4),
        cost_estimate=pl.CostEstimate(flops=0, bytes_accessed=8 * hidden * width, transcendentals=0),
        name="stage",
    )(in_hbm(w_held))
    far_rows = within_plane(picked)
    near_rows[3], staged = lax.optimization_barrier((near_rows[3], staged))
    got = near_rows + far_rows
    for i in range(1, parts):
        got += [across(v, i) for v in near_rows]
        got += [across(v, i) if d else first[i - 1] for d, v in enumerate(far_rows)]
    pieces = len(got)

    big = params(30)
    outs = pl.pallas_call(
        lambda *r: expert_kernel(parts, pieces, *r),
        out_shape=[sd((slots, width + LANES), BF16)] * parts + [sd((total, hidden), BF16)] * 3,
        in_specs=[VMEM] * (pieces + 2),
        out_specs=[VMEM] * (parts + 3),
        compiler_params=big,
        name="expert",
    )(*got, staged, w_down)
    dx_parts, (gg, gu, act) = outs[:parts], outs[parts:]
    returned = [dx_parts[0]] + [across(dx_parts[i], -i) for i in range(1, parts)]
    summed = pl.pallas_call(
        lambda *r: add_kernel(capacity, *r),
        out_shape=sd((devices, 2 * capacity, width + LANES), BF16),
        in_specs=[SMEM] + [VMEM] * parts,
        out_specs=VMEM,
        compiler_params=params(12),
        name="add",
    )(me, *returned)
    back = within_half(summed).reshape(slots, width + LANES)
    grad_gu, grad_down = pl.pallas_call(
        lambda *r: weights_kernel(pieces, *r),
        out_shape=[sd(w_gate_up.shape, BF16), sd(w_down.shape, BF16)],
        in_specs=[VMEM] * (pieces + 3),
        out_specs=[ANY] * 2,
        scratch_shapes=[
            pltpu.VMEM((3, hidden, width), BF16),
            pltpu.SemaphoreType.DMA((3, -(-hidden // LANES))),
        ],
        compiler_params=params(40),
        cost_estimate=pl.CostEstimate(
            flops=6 * hidden * total * width,
            bytes_accessed=10 * hidden * width,
            transcendentals=0,
        ),
        name="weights",
    )(*got, gg, gu, act)
    own_sum, far_sum = pl.pallas_call(
        lambda *r: combine_kernel(top, capacity, *r),
        out_shape=[sd((rows, width + LANES), F32), sd((rows, width + LANES), BF16)],
        in_specs=[SMEM] + [VMEM] * 3,
        out_specs=[VMEM] * 2,
        compiler_params=params(8),
        name="combine",
    )(half, back, own, far)
    home = mirror(far_sum)
    grad_tokens, grad_probs = pl.pallas_call(
        final_kernel,
        out_shape=[sd((rows, width), BF16), sd((top, rows), F32)],
        in_specs=[VMEM] * 2,
        out_specs=[VMEM] * 2,
        compiler_params=params(4),
        name="final",
    )(own_sum, home)
    return grad_tokens, grad_probs.T, grad_gu, grad_down


def solution(mesh):
    groups, columns = mesh.devices.shape
    every = ("seq", "zh", "zl", "slice")
    split = Mesh(mesh.devices.reshape(groups, 2, 2, columns // 4), every)

    def spec(rank):
        return P(every, *([None] * (rank - 1)))

    return jax.shard_map(
        body,
        mesh=split,
        in_specs=(spec(2), spec(2), spec(2), spec(2), spec(4), spec(3)),
        out_specs=(spec(2), spec(2), spec(4), spec(3)),
        check_vma=False,
    )
```

```python
import jax
import jax.numpy as jnp
from jax import lax
from jax.experimental import pallas as pl
from jax.experimental.pallas import tpu as pltpu
from jax.sharding import Mesh
from jax.sharding import PartitionSpec as P

LANES = 128
F32, BF16 = jnp.float32, jnp.bfloat16


def dot(a, b, ca, cb):
    return lax.dot_general(a, b, (((ca,), (cb,)), ((), ())), preferred_element_type=F32)


def lane_map(count, start):
    row = lax.broadcasted_iota(jnp.int32, (count, LANES), 0)
    lane = lax.broadcasted_iota(jnp.int32, (count, LANES), 1)
    return (lane == row + start).astype(BF16)


def held_slots(meta, top, expert, place):
    rows = meta.shape[0]
    match = [meta[:, k : k + 1] == expert for k in range(top)]
    named = jnp.zeros(expert.shape, F32)
    for m in match:
        named = named + m.astype(F32)
    earlier = lax.broadcasted_iota(jnp.int32, (rows, rows), 1) < lax.broadcasted_iota(
        jnp.int32, (rows, rows), 0
    )
    rank = dot(earlier.astype(BF16), named.astype(BF16), 1, 0)
    return match, jnp.where(rank == place, named, 0.0)


def pack_kernel(x_hbm, dy_hbm, ids_hbm, p_hbm, out_ref, ids_ref, p_ref, sems):
    width, top = x_hbm.shape[1], ids_ref.shape[0]
    small = [
        pltpu.make_async_copy(ids_hbm, ids_ref, sems.at[2]),
        pltpu.make_async_copy(p_hbm, p_ref, sems.at[3]),
    ]
    copies = [
        pltpu.make_async_copy(x_hbm, out_ref.at[:, pl.ds(0, width)], sems.at[0]),
        pltpu.make_async_copy(dy_hbm, out_ref.at[:, pl.ds(width, width)], sems.at[1]),
    ]
    for c in small + copies:
        c.start()
    for c in small:
        c.wait()
    ids = ids_ref[...].astype(F32).astype(BF16)
    meta = dot(ids, lane_map(top, 0), 0, 0) + dot(p_ref[...], lane_map(top, top), 0, 0)
    out_ref[:, 2 * width :] = meta.astype(BF16)
    for c in copies:
        c.wait()


def stage_kernel(src_hbm, out_ref, sem):
    copy = pltpu.make_async_copy(src_hbm, out_ref, sem)
    copy.start()
    copy.wait()


def select_kernel(top, capacity, half_ref, me_ref, first_ref, second_ref, *out_refs):
    width, size = (first_ref.shape[1] - LANES) // 2, 2 * capacity
    lane = lax.broadcasted_iota(jnp.int32, (first_ref.shape[0], len(out_refs) * size), 1)
    plane = (me_ref[0] // 2) ^ (lane // size)
    expert = (plane * 4 + half_ref[0] * 2 + me_ref[0] % 2).astype(F32)
    place = (lane % capacity).astype(F32)
    picks, weighted = [], []
    for which, ref in enumerate((first_ref, second_ref)):
        meta = ref[:, 2 * width :].astype(F32)
        match, held = held_slots(meta, top, expert, place)
        held = jnp.where((lane // capacity) % 2 == which, held, 0.0)
        weight = jnp.zeros(held.shape, F32)
        for k in range(top):
            weight = weight + jnp.where(match[k], meta[:, top + k : top + k + 1], 0.0)
        picks.append(held)
        weighted.append(held * weight)
    pick = jnp.concatenate(picks, 0).astype(BF16)
    rows = jnp.concatenate([first_ref[:, : 2 * width], second_ref[:, : 2 * width]], 0)
    rows = dot(pick, rows, 0, 0).astype(BF16)
    ones = jnp.ones((pick.shape[0], LANES), BF16)
    weight = dot(jnp.concatenate(weighted, 0).astype(BF16), ones, 0, 0).astype(BF16)
    for i, out_ref in enumerate(out_refs):
        out_ref[:, : 2 * width] = rows[i * size : (i + 1) * size]
        out_ref[:, 2 * width :] = weight[i * size : (i + 1) * size]


def expert_kernel(parts, pieces, *refs):
    got = refs[:pieces]
    wgu_ref, wd_ref = refs[pieces : pieces + 2]
    dx_out = refs[pieces + 2 : pieces + 2 + parts]
    gg_ref, gu_ref, act_ref = refs[pieces + 2 + parts :]
    width, slots = wd_ref.shape[2], dx_out[0].shape[0]
    xs = jnp.concatenate([r[:, :width] for r in got], 0)
    dys = jnp.concatenate([r[:, width : 2 * width] for r in got], 0)
    weight = jnp.concatenate([r[:, 2 * width :] for r in got], 0).astype(F32)[:, 0:1]
    gate = dot(xs, wgu_ref[0, 0], 1, 1)
    upper = dot(xs, wgu_ref[0, 1], 1, 1)
    err = dot(dys, wd_ref[0], 1, 1)
    sig = jax.nn.sigmoid(gate)
    silu = gate * sig
    act = silu * upper
    score = jnp.sum(err * act, axis=1, keepdims=True)
    delta = weight * err
    gg = (delta * upper * sig * (1.0 + gate * (1.0 - sig))).astype(BF16)
    gu = (delta * silu).astype(BF16)
    gg_ref[...] = gg
    gu_ref[...] = gu
    act_ref[...] = act.astype(BF16)
    score_col = jnp.broadcast_to(score, (score.shape[0], LANES)).astype(BF16)
    dx = (dot(gg, wgu_ref[0, 0], 1, 0) + dot(gu, wgu_ref[0, 1], 1, 0)).astype(BF16)
    for i in range(parts):
        dx_out[i][:, :width] = dx[i * slots : (i + 1) * slots]
        dx_out[i][:, width:] = score_col[i * slots : (i + 1) * slots]


def weights_kernel(parts, *refs):
    got = refs[:parts]
    gg_ref, gu_ref, act_ref, dgu_hbm, dd_hbm, buf, sems = refs[parts:]
    hidden, width = buf.shape[1:]
    xs = jnp.concatenate([r[:, :width] for r in got], 0)
    weight = jnp.concatenate([r[:, 2 * width :] for r in got], 0).astype(F32)[:, 0:1]
    dys = jnp.concatenate([r[:, width : 2 * width] for r in got], 0)
    scaled = (weight * dys.astype(F32)).astype(BF16)
    outs = ((gg_ref, xs, dgu_hbm.at[0, 0]), (gu_ref, xs, dgu_hbm.at[0, 1]), (act_ref, scaled, dd_hbm.at[0]))
    copies = []
    for i, (lhs_ref, rhs, out) in enumerate(outs):
        for j, start in enumerate(range(0, hidden, LANES)):
            size = min(LANES, hidden - start)
            buf[i, start : start + size, :] = dot(lhs_ref[:, start : start + size], rhs, 0, 0).astype(BF16)
            cut = pl.ds(start, size)
            copies.append(pltpu.make_async_copy(buf.at[i, cut], out.at[cut], sems.at[i, j]))
            copies[-1].start()
    for c in copies:
        c.wait()


def add_kernel(capacity, me_ref, *refs):
    out_ref = refs[-1]
    total = refs[0][...].astype(F32)
    for r in refs[1:-1]:
        total = total + r[...].astype(F32)
    total = total.astype(BF16)
    devices = out_ref.shape[0]
    for i in range(devices):
        near, far = (total[j * capacity : (j + 1) * capacity] for j in (i, devices + i))
        out_ref[me_ref[0] ^ i] = jnp.concatenate([near, far], 0)


def combine_kernel(top, capacity, half_ref, back_ref, own_ref, far_ref, own_out, far_out):
    slots, width = back_ref.shape[0], back_ref.shape[1] - LANES
    rows = own_ref.shape[0]
    lane = lax.broadcasted_iota(jnp.int32, (rows, LANES), 1)
    slot = lax.broadcasted_iota(jnp.int32, (rows, slots), 1)
    device = slot // (2 * capacity)
    expert = ((device // 2) * 4 + half_ref[0] * 2 + device % 2).astype(F32)
    place = (slot % capacity).astype(F32)
    for which, (meta_ref, out_ref) in enumerate(((own_ref, own_out), (far_ref, far_out))):
        meta = meta_ref[:, 2 * width :].astype(F32)
        match, held = held_slots(meta, top, expert, place)
        held = jnp.where((slot // capacity) % 2 == which, held, 0.0)
        dx = dot(held.astype(BF16), back_ref[:, :width], 1, 0)
        probs = jnp.zeros(lane.shape, F32)
        for k in range(top):
            one = jnp.where(match[k], held, 0.0).astype(BF16)
            probs = jnp.where(lane == k, dot(one, back_ref[:, width:], 1, 0), probs)
        out_ref[:, :width] = dx.astype(out_ref.dtype)
        out_ref[:, width:] = probs.astype(out_ref.dtype)


def final_kernel(own_ref, far_ref, dx_ref, dp_ref):
    width, top = dx_ref.shape[1], dp_ref.shape[0]
    dx_ref[...] = (own_ref[:, :width] + far_ref[:, :width].astype(F32)).astype(BF16)
    probs = (own_ref[:, width:] + far_ref[:, width:].astype(F32)).astype(BF16)
    dp_ref[...] = dot(lane_map(top, 0), probs, 1, 1)


def in_hbm(v):
    return pltpu.with_memory_space_constraint(v, pltpu.HBM)


def params(mib):
    return pltpu.CompilerParams(vmem_limit_bytes=mib * 1024 * 1024)


VMEM = pl.BlockSpec(memory_space=pltpu.VMEM)
SMEM = pl.BlockSpec(memory_space=pltpu.SMEM)
ANY = pl.BlockSpec(memory_space=pl.ANY)
HBM = pl.BlockSpec(memory_space=pltpu.HBM)


def body(tokens, out_grads, route_ids, route_probs, w_gate_up, w_down):
    rows, width = tokens.shape
    top = route_ids.shape[1]
    groups, parts = lax.axis_size("seq"), lax.axis_size("slice")
    experts = groups * 4
    hidden = w_down.shape[1]
    capacity = max(2, (rows * top * 4 // 3 + experts - 1) // experts)
    devices = groups * 2
    slots = devices * 2 * capacity
    total = slots * parts
    sd = jax.ShapeDtypeStruct

    def within_half(v):
        return lax.all_to_all(v, ("seq", "zl"), split_axis=0, concat_axis=0, tiled=True)

    def within_plane(pieces):
        order = [d for d in reversed(range(1, groups))]
        moved = list(pieces)
        for d in order:
            moved[d] = lax.ppermute(pieces[d], "seq", [(i, i ^ d) for i in range(groups)])
        return moved

    def across_half(v):
        return lax.ppermute(v, ("zh", "zl"), [(i, i ^ 2) for i in range(4)])

    def beside(v):
        return lax.ppermute(v, "zl", [(0, 1), (1, 0)])

    def mirror(v):
        return lax.ppermute(v, ("zh", "zl"), [(i, 3 - i) for i in range(4)])

    def across(v, step):
        return lax.ppermute(v, "slice", [(i, (i + step) % parts) for i in range(parts)])

    half = lax.axis_index("zh").astype(jnp.int32).reshape(1)
    me = lax.axis_index(("seq", "zl")).astype(jnp.int32).reshape(1)
    own = pl.pallas_call(
        pack_kernel,
        out_shape=pltpu.VMEM((rows, 2 * width + LANES), BF16),
        in_specs=[HBM] * 4,
        out_specs=VMEM,
        scratch_shapes=[
            pltpu.VMEM((top, rows), jnp.int32),
            pltpu.VMEM((top, rows), BF16),
            pltpu.SemaphoreType.DMA((4,)),
        ],
        compiler_params=params(4),
        name="pack",
    )(*[in_hbm(v) for v in (tokens, out_grads, route_ids.T, route_probs.T)])
    def select(first, second, name):
        return pl.pallas_call(
            lambda *r: select_kernel(top, capacity, *r),
            out_shape=[sd((2 * capacity, 2 * width + LANES), BF16)] * groups,
            in_specs=[SMEM, SMEM, VMEM, VMEM],
            out_specs=[VMEM] * groups,
            compiler_params=params(8),
            name=name,
        )(half, me, first, second)

    far = mirror(own)
    near = beside(own)
    beyond = across_half(own)
    picked = select(own, near, "near")
    near_rows = within_plane(picked)
    picked = select(far, beyond, "far")
    w_held, _ = lax.optimization_barrier((w_gate_up, picked))
    staged = pl.pallas_call(
        stage_kernel,
        out_shape=pltpu.VMEM(w_gate_up.shape, BF16),
        in_specs=[HBM],
        out_specs=VMEM,
        scratch_shapes=[pltpu.SemaphoreType.DMA],
        compiler_params=params(4),
        cost_estimate=pl.CostEstimate(flops=0, bytes_accessed=8 * hidden * width, transcendentals=0),
        name="stage",
    )(in_hbm(w_held))
    far_rows = within_plane(picked)
    near_rows[3], staged = lax.optimization_barrier((near_rows[3], staged))
    got = near_rows + far_rows
    for i in range(1, parts):
        got += [across(v, i) for v in near_rows]
        got += [across(v, i) for v in far_rows]
    pieces = len(got)

    big = params(30)
    outs = pl.pallas_call(
        lambda *r: expert_kernel(parts, pieces, *r),
        out_shape=[sd((slots, width + LANES), BF16)] * parts + [sd((total, hidden), BF16)] * 3,
        in_specs=[VMEM] * (pieces + 2),
        out_specs=[VMEM] * (parts + 3),
        compiler_params=big,
        name="expert",
    )(*got, staged, w_down)
    dx_parts, (gg, gu, act) = outs[:parts], outs[parts:]
    returned = [dx_parts[0]] + [across(dx_parts[i], -i) for i in range(1, parts)]
    summed = pl.pallas_call(
        lambda *r: add_kernel(capacity, *r),
        out_shape=sd((devices, 2 * capacity, width + LANES), BF16),
        in_specs=[SMEM] + [VMEM] * parts,
        out_specs=VMEM,
        compiler_params=params(12),
        name="add",
    )(me, *returned)
    back = within_half(summed).reshape(slots, width + LANES)
    grad_gu, grad_down = pl.pallas_call(
        lambda *r: weights_kernel(pieces, *r),
        out_shape=[sd(w_gate_up.shape, BF16), sd(w_down.shape, BF16)],
        in_specs=[VMEM] * (pieces + 3),
        out_specs=[ANY] * 2,
        scratch_shapes=[
            pltpu.VMEM((3, hidden, width), BF16),
            pltpu.SemaphoreType.DMA((3, -(-hidden // LANES))),
        ],
        compiler_params=params(40),
        cost_estimate=pl.CostEstimate(
            flops=6 * hidden * total * width,
            bytes_accessed=10 * hidden * width,
            transcendentals=0,
        ),
        name="weights",
    )(*got, gg, gu, act)
    own_sum, far_sum = pl.pallas_call(
        lambda *r: combine_kernel(top, capacity, *r),
        out_shape=[sd((rows, width + LANES), F32), sd((rows, width + LANES), BF16)],
        in_specs=[SMEM] + [VMEM] * 3,
        out_specs=[VMEM] * 2,
        compiler_params=params(8),
        name="combine",
    )(half, back, own, far)
    home = mirror(far_sum)
    grad_tokens, grad_probs = pl.pallas_call(
        final_kernel,
        out_shape=[sd((rows, width), BF16), sd((top, rows), F32)],
        in_specs=[VMEM] * 2,
        out_specs=[VMEM] * 2,
        compiler_params=params(4),
        name="final",
    )(own_sum, home)
    return grad_tokens, grad_probs.T, grad_gu, grad_down


def solution(mesh):
    groups, columns = mesh.devices.shape
    every = ("seq", "zh", "zl", "slice")
    split = Mesh(mesh.devices.reshape(groups, 2, 2, columns // 4), every)

    def spec(rank):
        return P(every, *([None] * (rank - 1)))

    return jax.shard_map(
        body,
        mesh=split,
        in_specs=(spec(2), spec(2), spec(2), spec(2), spec(4), spec(3)),
        out_specs=(spec(2), spec(2), spec(4), spec(3)),
        check_vma=False,
    )
```

```python
import jax
import jax.numpy as jnp
from jax import lax
from jax.experimental import pallas as pl
from jax.experimental.pallas import tpu as pltpu
from jax.sharding import Mesh
from jax.sharding import PartitionSpec as P

LANES = 128
F32, BF16 = jnp.float32, jnp.bfloat16


def dot(a, b, ca, cb):
    return lax.dot_general(a, b, (((ca,), (cb,)), ((), ())), preferred_element_type=F32)


def lane_map(count, start):
    row = lax.broadcasted_iota(jnp.int32, (count, LANES), 0)
    lane = lax.broadcasted_iota(jnp.int32, (count, LANES), 1)
    return (lane == row + start).astype(BF16)


def held_slots(meta, top, expert, place):
    rows = meta.shape[0]
    match = [meta[:, k : k + 1] == expert for k in range(top)]
    named = jnp.zeros(expert.shape, F32)
    for m in match:
        named = named + m.astype(F32)
    earlier = lax.broadcasted_iota(jnp.int32, (rows, rows), 1) < lax.broadcasted_iota(
        jnp.int32, (rows, rows), 0
    )
    rank = dot(earlier.astype(BF16), named.astype(BF16), 1, 0)
    return match, jnp.where(rank == place, named, 0.0)


def pack_kernel(x_hbm, dy_hbm, ids_hbm, p_hbm, out_ref, ids_ref, p_ref, sems):
    width, top = x_hbm.shape[1], ids_ref.shape[0]
    small = [
        pltpu.make_async_copy(ids_hbm, ids_ref, sems.at[2]),
        pltpu.make_async_copy(p_hbm, p_ref, sems.at[3]),
    ]
    copies = [
        pltpu.make_async_copy(x_hbm, out_ref.at[:, pl.ds(0, width)], sems.at[0]),
        pltpu.make_async_copy(dy_hbm, out_ref.at[:, pl.ds(width, width)], sems.at[1]),
    ]
    for c in small + copies:
        c.start()
    for c in small:
        c.wait()
    ids = ids_ref[...].astype(F32).astype(BF16)
    meta = dot(ids, lane_map(top, 0), 0, 0) + dot(p_ref[...], lane_map(top, top), 0, 0)
    out_ref[:, 2 * width :] = meta.astype(BF16)
    for c in copies:
        c.wait()


def stage_kernel(src_hbm, out_ref, sem):
    copy = pltpu.make_async_copy(src_hbm, out_ref, sem)
    copy.start()
    copy.wait()


def select_kernel(top, capacity, half_ref, me_ref, first_ref, second_ref, *out_refs):
    width, size = (first_ref.shape[1] - LANES) // 2, 2 * capacity
    lane = lax.broadcasted_iota(jnp.int32, (first_ref.shape[0], len(out_refs) * size), 1)
    plane = (me_ref[0] // 2) ^ (lane // size)
    expert = (plane * 4 + half_ref[0] * 2 + me_ref[0] % 2).astype(F32)
    place = (lane % capacity).astype(F32)
    picks, weighted = [], []
    for which, ref in enumerate((first_ref, second_ref)):
        meta = ref[:, 2 * width :].astype(F32)
        match, held = held_slots(meta, top, expert, place)
        held = jnp.where((lane // capacity) % 2 == which, held, 0.0)
        weight = jnp.zeros(held.shape, F32)
        for k in range(top):
            weight = weight + jnp.where(match[k], meta[:, top + k : top + k + 1], 0.0)
        picks.append(held)
        weighted.append(held * weight)
    pick = jnp.concatenate(picks, 0).astype(BF16)
    rows = jnp.concatenate([first_ref[:, : 2 * width], second_ref[:, : 2 * width]], 0)
    rows = dot(pick, rows, 0, 0).astype(BF16)
    ones = jnp.ones((pick.shape[0], LANES), BF16)
    weight = dot(jnp.concatenate(weighted, 0).astype(BF16), ones, 0, 0).astype(BF16)
    for i, out_ref in enumerate(out_refs):
        out_ref[:, : 2 * width] = rows[i * size : (i + 1) * size]
        out_ref[:, 2 * width :] = weight[i * size : (i + 1) * size]


def expert_kernel(parts, pieces, *refs):
    got = refs[:pieces]
    wgu_ref, wd_ref = refs[pieces : pieces + 2]
    dx_out = refs[pieces + 2 : pieces + 2 + parts]
    gg_ref, gu_ref, act_ref = refs[pieces + 2 + parts :]
    width, slots = wd_ref.shape[2], dx_out[0].shape[0]
    xs = jnp.concatenate([r[:, :width] for r in got], 0)
    dys = jnp.concatenate([r[:, width : 2 * width] for r in got], 0)
    weight = jnp.concatenate([r[:, 2 * width :] for r in got], 0).astype(F32)[:, 0:1]
    gate = dot(xs, wgu_ref[0, 0], 1, 1)
    upper = dot(xs, wgu_ref[0, 1], 1, 1)
    err = dot(dys, wd_ref[0], 1, 1)
    sig = jax.nn.sigmoid(gate)
    silu = gate * sig
    act = silu * upper
    score = jnp.sum(err * act, axis=1, keepdims=True)
    delta = weight * err
    gg = (delta * upper * sig * (1.0 + gate * (1.0 - sig))).astype(BF16)
    gu = (delta * silu).astype(BF16)
    gg_ref[...] = gg
    gu_ref[...] = gu
    act_ref[...] = act.astype(BF16)
    score_col = jnp.broadcast_to(score, (score.shape[0], LANES)).astype(BF16)
    dx = (dot(gg, wgu_ref[0, 0], 1, 0) + dot(gu, wgu_ref[0, 1], 1, 0)).astype(BF16)
    for i in range(parts):
        dx_out[i][:, :width] = dx[i * slots : (i + 1) * slots]
        dx_out[i][:, width:] = score_col[i * slots : (i + 1) * slots]


def weights_kernel(parts, *refs):
    got = refs[:parts]
    gg_ref, gu_ref, act_ref, dgu_hbm, dd_hbm, buf, sems = refs[parts:]
    hidden, width = buf.shape[1:]
    xs = jnp.concatenate([r[:, :width] for r in got], 0)
    weight = jnp.concatenate([r[:, 2 * width :] for r in got], 0).astype(F32)[:, 0:1]
    dys = jnp.concatenate([r[:, width : 2 * width] for r in got], 0)
    scaled = (weight * dys.astype(F32)).astype(BF16)
    outs = ((gg_ref, xs, dgu_hbm.at[0, 0]), (gu_ref, xs, dgu_hbm.at[0, 1]), (act_ref, scaled, dd_hbm.at[0]))
    copies = []
    for i, (lhs_ref, rhs, out) in enumerate(outs):
        for j, start in enumerate(range(0, hidden, LANES)):
            size = min(LANES, hidden - start)
            buf[i, start : start + size, :] = dot(lhs_ref[:, start : start + size], rhs, 0, 0).astype(BF16)
            cut = pl.ds(start, size)
            copies.append(pltpu.make_async_copy(buf.at[i, cut], out.at[cut], sems.at[i, j]))
            copies[-1].start()
    for c in copies:
        c.wait()


def add_kernel(parts, *refs):
    outs = refs[parts:]
    total = refs[0][...].astype(F32)
    for r in refs[1:parts]:
        total = total + r[...].astype(F32)
    total = total.astype(BF16)
    size = outs[0].shape[0]
    for i, out_ref in enumerate(outs):
        out_ref[...] = total[i * size : (i + 1) * size]


def combine_kernel(top, capacity, pieces, half_ref, me_ref, *refs):
    back = jnp.concatenate([r[...] for r in refs[:pieces]], 0)
    metas, outs = refs[pieces : pieces + 2], refs[pieces + 2 :]
    slots, width = back.shape[0], back.shape[1] - LANES
    rows = metas[0].shape[0]
    lane = lax.broadcasted_iota(jnp.int32, (rows, LANES), 1)
    slot = lax.broadcasted_iota(jnp.int32, (rows, slots), 1)
    plane = (me_ref[0] // 2) ^ (slot // (2 * capacity))
    expert = (plane * 4 + half_ref[0] * 2 + me_ref[0] % 2).astype(F32)
    place = (slot % capacity).astype(F32)
    masks, routes = [], []
    for which, meta_ref in enumerate(metas):
        meta = meta_ref[:, 2 * width :].astype(F32)
        match, held = held_slots(meta, top, expert, place)
        held = jnp.where((slot // capacity) % 2 == which, held, 0.0)
        masks.append(held)
        routes += [jnp.where(m, held, 0.0) for m in match]
    dx = dot(jnp.concatenate(masks, 0).astype(BF16), back[:, :width], 1, 0)
    scores = dot(jnp.concatenate(routes, 0).astype(BF16), back[:, width:], 1, 0)
    for i, out_ref in enumerate(outs):
        probs = jnp.zeros(lane.shape, F32)
        for k in range(top):
            start = (i * top + k) * rows
            probs = jnp.where(lane == k, scores[start : start + rows], probs)
        out_ref[:, :width] = dx[i * rows : (i + 1) * rows].astype(out_ref.dtype)
        out_ref[:, width:] = probs.astype(out_ref.dtype)


def final_kernel(own_ref, *refs):
    dx_ref, dp_ref = refs[-2:]
    width, top = dx_ref.shape[1], dp_ref.shape[0]
    total = own_ref[...]
    for r in refs[:-2]:
        total = total + r[...].astype(F32)
    dx_ref[...] = total[:, :width].astype(BF16)
    dp_ref[...] = dot(lane_map(top, 0), total[:, width:].astype(BF16), 1, 1)


def in_hbm(v):
    return pltpu.with_memory_space_constraint(v, pltpu.HBM)


def params(mib):
    return pltpu.CompilerParams(vmem_limit_bytes=mib * 1024 * 1024)


VMEM = pl.BlockSpec(memory_space=pltpu.VMEM)
SMEM = pl.BlockSpec(memory_space=pltpu.SMEM)
ANY = pl.BlockSpec(memory_space=pl.ANY)
HBM = pl.BlockSpec(memory_space=pltpu.HBM)


def body(tokens, out_grads, route_ids, route_probs, w_gate_up, w_down):
    rows, width = tokens.shape
    top = route_ids.shape[1]
    groups, parts = lax.axis_size("seq"), lax.axis_size("slice")
    experts = groups * 4
    hidden = w_down.shape[1]
    capacity = max(2, (rows * top * 4 // 3 + experts - 1) // experts)
    devices = groups * 2
    slots = devices * 2 * capacity
    total = slots * parts
    sd = jax.ShapeDtypeStruct

    def within_plane(pieces):
        order = [d for d in reversed(range(1, groups))]
        moved = list(pieces)
        for d in order:
            moved[d] = lax.ppermute(pieces[d], "seq", [(i, i ^ d) for i in range(groups)])
        return moved

    def across_half(v):
        return lax.ppermute(v, ("zh", "zl"), [(i, i ^ 2) for i in range(4)])

    def beside(v):
        return lax.ppermute(v, "zl", [(0, 1), (1, 0)])

    def mirror(v):
        return lax.ppermute(v, ("zh", "zl"), [(i, 3 - i) for i in range(4)])

    def across(v, step):
        return lax.ppermute(v, "slice", [(i, (i + step) % parts) for i in range(parts)])

    half = lax.axis_index("zh").astype(jnp.int32).reshape(1)
    me = lax.axis_index(("seq", "zl")).astype(jnp.int32).reshape(1)
    own = pl.pallas_call(
        pack_kernel,
        out_shape=pltpu.VMEM((rows, 2 * width + LANES), BF16),
        in_specs=[HBM] * 4,
        out_specs=VMEM,
        scratch_shapes=[
            pltpu.VMEM((top, rows), jnp.int32),
            pltpu.VMEM((top, rows), BF16),
            pltpu.SemaphoreType.DMA((4,)),
        ],
        compiler_params=params(4),
        name="pack",
    )(*[in_hbm(v) for v in (tokens, out_grads, route_ids.T, route_probs.T)])
    def select(first, second, name):
        return pl.pallas_call(
            lambda *r: select_kernel(top, capacity, *r),
            out_shape=[sd((2 * capacity, 2 * width + LANES), BF16)] * groups,
            in_specs=[SMEM, SMEM, VMEM, VMEM],
            out_specs=[VMEM] * groups,
            compiler_params=params(8),
            name=name,
        )(half, me, first, second)

    far = mirror(own)
    near = beside(own)
    beyond = across_half(own)
    picked = select(own, near, "near")
    near_rows = within_plane(picked)
    picked = select(far, beyond, "far")
    w_held, _ = lax.optimization_barrier((w_gate_up, picked))
    staged = pl.pallas_call(
        stage_kernel,
        out_shape=pltpu.VMEM(w_gate_up.shape, BF16),
        in_specs=[HBM],
        out_specs=VMEM,
        scratch_shapes=[pltpu.SemaphoreType.DMA],
        compiler_params=params(4),
        cost_estimate=pl.CostEstimate(flops=0, bytes_accessed=8 * hidden * width, transcendentals=0),
        name="stage",
    )(in_hbm(w_held))
    far_rows = within_plane(picked)
    near_rows[3], staged = lax.optimization_barrier((near_rows[3], staged))
    got = near_rows + far_rows
    for i in range(1, parts):
        got += [across(v, i) for v in near_rows]
        got += [across(v, i) for v in far_rows]
    pieces = len(got)

    big = params(30)
    outs = pl.pallas_call(
        lambda *r: expert_kernel(parts, pieces, *r),
        out_shape=[sd((slots, width + LANES), BF16)] * parts + [sd((total, hidden), BF16)] * 3,
        in_specs=[VMEM] * (pieces + 2),
        out_specs=[VMEM] * (parts + 3),
        compiler_params=big,
        name="expert",
    )(*got, staged, w_down)
    dx_parts, (gg, gu, act) = outs[:parts], outs[parts:]
    returned = [dx_parts[0]] + [across(dx_parts[i], -i) for i in range(1, parts)]
    summed = pl.pallas_call(
        lambda *r: add_kernel(parts, *r),
        out_shape=[sd((2 * capacity, width + LANES), BF16)] * (2 * groups),
        in_specs=[VMEM] * parts,
        out_specs=[VMEM] * (2 * groups),
        compiler_params=params(12),
        name="add",
    )(*returned)
    far_back, near_back = within_plane(summed[groups:]), within_plane(summed[:groups])
    grad_gu, grad_down = pl.pallas_call(
        lambda *r: weights_kernel(pieces, *r),
        out_shape=[sd(w_gate_up.shape, BF16), sd(w_down.shape, BF16)],
        in_specs=[VMEM] * (pieces + 3),
        out_specs=[ANY] * 2,
        scratch_shapes=[
            pltpu.VMEM((3, hidden, width), BF16),
            pltpu.SemaphoreType.DMA((3, -(-hidden // LANES))),
        ],
        compiler_params=params(40),
        cost_estimate=pl.CostEstimate(
            flops=6 * hidden * total * width,
            bytes_accessed=10 * hidden * width,
            transcendentals=0,
        ),
        name="weights",
    )(*got, gg, gu, act)

    def combine(back, blocks, types, name):
        return pl.pallas_call(
            lambda *r: combine_kernel(top, capacity, groups, *r),
            out_shape=[sd((rows, width + LANES), t) for t in types],
            in_specs=[SMEM] * 2 + [VMEM] * (groups + 2),
            out_specs=[VMEM] * 2,
            compiler_params=params(12),
            name=name,
        )(half, me, *back, *blocks)

    far_sum, beyond_sum = combine(far_back, (far, beyond), (BF16, BF16), "combine_far")
    near_back[0], _ = lax.optimization_barrier((near_back[0], far_sum))
    own_sum, near_sum = combine(near_back, (own, near), (F32, BF16), "combine_near")
    home = [mirror(far_sum), across_half(beyond_sum), beside(near_sum)]
    grad_tokens, grad_probs = pl.pallas_call(
        final_kernel,
        out_shape=[sd((rows, width), BF16), sd((top, rows), F32)],
        in_specs=[VMEM] * 4,
        out_specs=[VMEM] * 2,
        compiler_params=params(4),
        name="final",
    )(own_sum, *home)
    return grad_tokens, grad_probs.T, grad_gu, grad_down


def solution(mesh):
    groups, columns = mesh.devices.shape
    every = ("seq", "zh", "zl", "slice")
    split = Mesh(mesh.devices.reshape(groups, 2, 2, columns // 4), every)

    def spec(rank):
        return P(every, *([None] * (rank - 1)))

    return jax.shard_map(
        body,
        mesh=split,
        in_specs=(spec(2), spec(2), spec(2), spec(2), spec(4), spec(3)),
        out_specs=(spec(2), spec(2), spec(4), spec(3)),
        check_vma=False,
    )
```

```python
import jax
import jax.numpy as jnp
from jax import lax
from jax.experimental import pallas as pl
from jax.experimental.pallas import tpu as pltpu
from jax.sharding import Mesh
from jax.sharding import PartitionSpec as P

LANES = 128
F32, BF16 = jnp.float32, jnp.bfloat16


def dot(a, b, ca, cb):
    return lax.dot_general(a, b, (((ca,), (cb,)), ((), ())), preferred_element_type=F32)


def lane_map(count, start):
    row = lax.broadcasted_iota(jnp.int32, (count, LANES), 0)
    lane = lax.broadcasted_iota(jnp.int32, (count, LANES), 1)
    return (lane == row + start).astype(BF16)


def held_slots(meta, top, expert, place):
    rows = meta.shape[0]
    match = [meta[:, k : k + 1] == expert for k in range(top)]
    named = jnp.zeros(expert.shape, F32)
    for m in match:
        named = named + m.astype(F32)
    earlier = lax.broadcasted_iota(jnp.int32, (rows, rows), 1) < lax.broadcasted_iota(
        jnp.int32, (rows, rows), 0
    )
    rank = dot(earlier.astype(BF16), named.astype(BF16), 1, 0)
    return match, jnp.where(rank == place, named, 0.0)


def pack_kernel(x_hbm, dy_hbm, ids_hbm, p_hbm, out_ref, ids_ref, p_ref, sems):
    width, top = x_hbm.shape[1], ids_ref.shape[0]
    small = [
        pltpu.make_async_copy(ids_hbm, ids_ref, sems.at[2]),
        pltpu.make_async_copy(p_hbm, p_ref, sems.at[3]),
    ]
    copies = [
        pltpu.make_async_copy(x_hbm, out_ref.at[:, pl.ds(0, width)], sems.at[0]),
        pltpu.make_async_copy(dy_hbm, out_ref.at[:, pl.ds(width, width)], sems.at[1]),
    ]
    for c in small + copies:
        c.start()
    for c in small:
        c.wait()
    ids = ids_ref[...].astype(F32).astype(BF16)
    meta = dot(ids, lane_map(top, 0), 0, 0) + dot(p_ref[...], lane_map(top, top), 0, 0)
    out_ref[:, 2 * width :] = meta.astype(BF16)
    for c in copies:
        c.wait()


def stage_kernel(src_hbm, out_ref, sem):
    copy = pltpu.make_async_copy(src_hbm, out_ref, sem)
    copy.start()
    copy.wait()


def select_kernel(top, capacity, half_ref, me_ref, first_ref, second_ref, *out_refs):
    width, size = (first_ref.shape[1] - LANES) // 2, 2 * capacity
    lane = lax.broadcasted_iota(jnp.int32, (first_ref.shape[0], len(out_refs) * size), 1)
    plane = (me_ref[0] // 2) ^ (lane // size)
    expert = (plane * 4 + half_ref[0] * 2 + me_ref[0] % 2).astype(F32)
    place = (lane % capacity).astype(F32)
    picks, weighted = [], []
    for which, ref in enumerate((first_ref, second_ref)):
        meta = ref[:, 2 * width :].astype(F32)
        match, held = held_slots(meta, top, expert, place)
        held = jnp.where((lane // capacity) % 2 == which, held, 0.0)
        weight = jnp.zeros(held.shape, F32)
        for k in range(top):
            weight = weight + jnp.where(match[k], meta[:, top + k : top + k + 1], 0.0)
        picks.append(held)
        weighted.append(held * weight)
    pick = jnp.concatenate(picks, 0).astype(BF16)
    rows = jnp.concatenate([first_ref[:, : 2 * width], second_ref[:, : 2 * width]], 0)
    rows = dot(pick, rows, 0, 0).astype(BF16)
    ones = jnp.ones((pick.shape[0], LANES), BF16)
    weight = dot(jnp.concatenate(weighted, 0).astype(BF16), ones, 0, 0).astype(BF16)
    for i, out_ref in enumerate(out_refs):
        out_ref[:, : 2 * width] = rows[i * size : (i + 1) * size]
        out_ref[:, 2 * width :] = weight[i * size : (i + 1) * size]


def expert_kernel(parts, pieces, *refs):
    got = refs[:pieces]
    wgu_ref, wd_ref = refs[pieces : pieces + 2]
    dx_out = refs[pieces + 2 : pieces + 2 + parts]
    gg_ref, gu_ref, act_ref = refs[pieces + 2 + parts :]
    width, slots = wd_ref.shape[2], dx_out[0].shape[0]
    xs = jnp.concatenate([r[:, :width] for r in got], 0)
    dys = jnp.concatenate([r[:, width : 2 * width] for r in got], 0)
    weight = jnp.concatenate([r[:, 2 * width :] for r in got], 0).astype(F32)[:, 0:1]
    gate = dot(xs, wgu_ref[0, 0], 1, 1)
    upper = dot(xs, wgu_ref[0, 1], 1, 1)
    err = dot(dys, wd_ref[0], 1, 1)
    sig = jax.nn.sigmoid(gate)
    silu = gate * sig
    act = silu * upper
    score = jnp.sum(err * act, axis=1, keepdims=True)
    delta = weight * err
    gg = (delta * upper * sig * (1.0 + gate * (1.0 - sig))).astype(BF16)
    gu = (delta * silu).astype(BF16)
    gg_ref[...] = gg
    gu_ref[...] = gu
    act_ref[...] = act.astype(BF16)
    score_col = jnp.broadcast_to(score, (score.shape[0], LANES)).astype(BF16)
    dx = (dot(gg, wgu_ref[0, 0], 1, 0) + dot(gu, wgu_ref[0, 1], 1, 0)).astype(BF16)
    for i in range(parts):
        dx_out[i][:, :width] = dx[i * slots : (i + 1) * slots]
        dx_out[i][:, width:] = score_col[i * slots : (i + 1) * slots]


def leave_in_chunks(lhs_ref, rhs, buf, out, sems):
    hidden, copies = buf.shape[0], []
    for j, start in enumerate(range(0, hidden, LANES)):
        cut = pl.ds(start, min(LANES, hidden - start))
        stop = min(start + LANES, hidden)
        buf[start:stop, :] = dot(lhs_ref[:, start:stop], rhs, 0, 0).astype(BF16)
        copies.append(pltpu.make_async_copy(buf.at[cut], out.at[cut], sems.at[j]))
        copies[-1].start()
    return copies


def gate_up_kernel(pieces, *refs):
    gg_ref, gu_ref, out_hbm, buf, sems = refs[pieces:]
    xs = jnp.concatenate([r[:, : buf.shape[2]] for r in refs[:pieces]], 0)
    copies = []
    for i, lhs_ref in enumerate((gg_ref, gu_ref)):
        copies += leave_in_chunks(lhs_ref, xs, buf.at[i], out_hbm.at[0, i], sems.at[i])
    for c in copies:
        c.wait()


def down_kernel(pieces, *refs):
    act_ref, out_hbm, buf, sems = refs[pieces:]
    got, width = refs[:pieces], buf.shape[1]
    weight = jnp.concatenate([r[:, 2 * width :] for r in got], 0).astype(F32)[:, 0:1]
    dys = jnp.concatenate([r[:, width : 2 * width] for r in got], 0)
    scaled = (weight * dys.astype(F32)).astype(BF16)
    for c in leave_in_chunks(act_ref, scaled, buf, out_hbm.at[0], sems):
        c.wait()


def add_kernel(parts, *refs):
    outs = refs[parts:]
    total = refs[0][...].astype(F32)
    for r in refs[1:parts]:
        total = total + r[...].astype(F32)
    total = total.astype(BF16)
    size = outs[0].shape[0]
    for i, out_ref in enumerate(outs):
        out_ref[...] = total[i * size : (i + 1) * size]


def combine_kernel(top, capacity, pieces, half_ref, me_ref, *refs):
    back = jnp.concatenate([r[...] for r in refs[:pieces]], 0)
    metas, outs = refs[pieces : pieces + 2], refs[pieces + 2 :]
    slots, width = back.shape[0], back.shape[1] - LANES
    rows = metas[0].shape[0]
    lane = lax.broadcasted_iota(jnp.int32, (rows, LANES), 1)
    slot = lax.broadcasted_iota(jnp.int32, (rows, slots), 1)
    plane = (me_ref[0] // 2) ^ (slot // (2 * capacity))
    expert = (plane * 4 + half_ref[0] * 2 + me_ref[0] % 2).astype(F32)
    place = (slot % capacity).astype(F32)
    masks, routes = [], []
    for which, meta_ref in enumerate(metas):
        meta = meta_ref[:, 2 * width :].astype(F32)
        match, held = held_slots(meta, top, expert, place)
        held = jnp.where((slot // capacity) % 2 == which, held, 0.0)
        masks.append(held)
        routes += [jnp.where(m, held, 0.0) for m in match]
    dx = dot(jnp.concatenate(masks, 0).astype(BF16), back[:, :width], 1, 0)
    scores = dot(jnp.concatenate(routes, 0).astype(BF16), back[:, width:], 1, 0)
    for i, out_ref in enumerate(outs):
        probs = jnp.zeros(lane.shape, F32)
        for k in range(top):
            start = (i * top + k) * rows
            probs = jnp.where(lane == k, scores[start : start + rows], probs)
        out_ref[:, :width] = dx[i * rows : (i + 1) * rows].astype(out_ref.dtype)
        out_ref[:, width:] = probs.astype(out_ref.dtype)


def final_kernel(own_ref, *refs):
    dx_ref, dp_ref = refs[-2:]
    width, top = dx_ref.shape[1], dp_ref.shape[0]
    total = own_ref[...]
    for r in refs[:-2]:
        total = total + r[...].astype(F32)
    dx_ref[...] = total[:, :width].astype(BF16)
    dp_ref[...] = dot(lane_map(top, 0), total[:, width:].astype(BF16), 1, 1)


def in_hbm(v):
    return pltpu.with_memory_space_constraint(v, pltpu.HBM)


def params(mib):
    return pltpu.CompilerParams(vmem_limit_bytes=mib * 1024 * 1024)


VMEM = pl.BlockSpec(memory_space=pltpu.VMEM)
SMEM = pl.BlockSpec(memory_space=pltpu.SMEM)
ANY = pl.BlockSpec(memory_space=pl.ANY)
HBM = pl.BlockSpec(memory_space=pltpu.HBM)


def body(tokens, out_grads, route_ids, route_probs, w_gate_up, w_down):
    rows, width = tokens.shape
    top = route_ids.shape[1]
    groups, parts = lax.axis_size("seq"), lax.axis_size("slice")
    experts = groups * 4
    hidden = w_down.shape[1]
    capacity = max(2, (rows * top * 4 // 3 + experts - 1) // experts)
    devices = groups * 2
    slots = devices * 2 * capacity
    total = slots * parts
    sd = jax.ShapeDtypeStruct

    def within_plane(pieces):
        order = [d for d in reversed(range(1, groups))]
        moved = list(pieces)
        for d in order:
            moved[d] = lax.ppermute(pieces[d], "seq", [(i, i ^ d) for i in range(groups)])
        return moved

    def across_half(v):
        return lax.ppermute(v, ("zh", "zl"), [(i, i ^ 2) for i in range(4)])

    def beside(v):
        return lax.ppermute(v, "zl", [(0, 1), (1, 0)])

    def mirror(v):
        return lax.ppermute(v, ("zh", "zl"), [(i, 3 - i) for i in range(4)])

    def across(v, step):
        return lax.ppermute(v, "slice", [(i, (i + step) % parts) for i in range(parts)])

    half = lax.axis_index("zh").astype(jnp.int32).reshape(1)
    me = lax.axis_index(("seq", "zl")).astype(jnp.int32).reshape(1)
    own = pl.pallas_call(
        pack_kernel,
        out_shape=pltpu.VMEM((rows, 2 * width + LANES), BF16),
        in_specs=[HBM] * 4,
        out_specs=VMEM,
        scratch_shapes=[
            pltpu.VMEM((top, rows), jnp.int32),
            pltpu.VMEM((top, rows), BF16),
            pltpu.SemaphoreType.DMA((4,)),
        ],
        compiler_params=params(4),
        name="pack",
    )(*[in_hbm(v) for v in (tokens, out_grads, route_ids.T, route_probs.T)])
    def select(first, second, name):
        return pl.pallas_call(
            lambda *r: select_kernel(top, capacity, *r),
            out_shape=[sd((2 * capacity, 2 * width + LANES), BF16)] * groups,
            in_specs=[SMEM, SMEM, VMEM, VMEM],
            out_specs=[VMEM] * groups,
            compiler_params=params(8),
            name=name,
        )(half, me, first, second)

    far = mirror(own)
    near = beside(own)
    beyond = across_half(own)
    picked = select(own, near, "near")
    near_rows = within_plane(picked)
    picked = select(far, beyond, "far")
    w_held, _ = lax.optimization_barrier((w_gate_up, picked))
    staged = pl.pallas_call(
        stage_kernel,
        out_shape=pltpu.VMEM(w_gate_up.shape, BF16),
        in_specs=[HBM],
        out_specs=VMEM,
        scratch_shapes=[pltpu.SemaphoreType.DMA],
        compiler_params=params(4),
        cost_estimate=pl.CostEstimate(flops=0, bytes_accessed=8 * hidden * width, transcendentals=0),
        name="stage",
    )(in_hbm(w_held))
    far_rows = within_plane(picked)
    near_rows[3], staged = lax.optimization_barrier((near_rows[3], staged))
    got = near_rows + far_rows
    for i in range(1, parts):
        got += [across(v, i) for v in near_rows]
        got += [across(v, i) for v in far_rows]
    pieces = len(got)

    big = params(30)
    outs = pl.pallas_call(
        lambda *r: expert_kernel(parts, pieces, *r),
        out_shape=[sd((slots, width + LANES), BF16)] * parts + [sd((total, hidden), BF16)] * 3,
        in_specs=[VMEM] * (pieces + 2),
        out_specs=[VMEM] * (parts + 3),
        compiler_params=big,
        name="expert",
    )(*got, staged, w_down)
    dx_parts, (gg, gu, act) = outs[:parts], outs[parts:]
    returned = [dx_parts[0]] + [across(dx_parts[i], -i) for i in range(1, parts)]
    grad_down = pl.pallas_call(
        lambda *r: down_kernel(pieces, *r),
        out_shape=sd(w_down.shape, BF16),
        in_specs=[VMEM] * (pieces + 1),
        out_specs=ANY,
        scratch_shapes=[pltpu.VMEM((hidden, width), BF16), pltpu.SemaphoreType.DMA((-(-hidden // LANES),))],
        compiler_params=params(30),
        cost_estimate=pl.CostEstimate(
            flops=2 * hidden * total * width, bytes_accessed=4 * hidden * width, transcendentals=0
        ),
        name="down",
    )(*got, act)
    returned[0], grad_down = lax.optimization_barrier((returned[0], grad_down))
    summed = pl.pallas_call(
        lambda *r: add_kernel(parts, *r),
        out_shape=[sd((2 * capacity, width + LANES), BF16)] * (2 * groups),
        in_specs=[VMEM] * parts,
        out_specs=[VMEM] * (2 * groups),
        compiler_params=params(12),
        name="add",
    )(*returned)
    far_back, near_back = within_plane(summed[groups:]), within_plane(summed[:groups])
    chunks = -(-hidden // LANES)
    grad_gu = pl.pallas_call(
        lambda *r: gate_up_kernel(pieces, *r),
        out_shape=sd(w_gate_up.shape, BF16),
        in_specs=[VMEM] * (pieces + 2),
        out_specs=ANY,
        scratch_shapes=[pltpu.VMEM((2, hidden, width), BF16), pltpu.SemaphoreType.DMA((2, chunks))],
        compiler_params=params(30),
        cost_estimate=pl.CostEstimate(
            flops=4 * hidden * total * width, bytes_accessed=8 * hidden * width, transcendentals=0
        ),
        name="gate_up",
    )(*got, gg, gu)

    def combine(back, blocks, types, name):
        return pl.pallas_call(
            lambda *r: combine_kernel(top, capacity, groups, *r),
            out_shape=[sd((rows, width + LANES), t) for t in types],
            in_specs=[SMEM] * 2 + [VMEM] * (groups + 2),
            out_specs=[VMEM] * 2,
            compiler_params=params(12),
            name=name,
        )(half, me, *back, *blocks)

    far_sum, beyond_sum = combine(far_back, (far, beyond), (BF16, BF16), "combine_far")
    near_back[0], _ = lax.optimization_barrier((near_back[0], far_sum))
    own_sum, near_sum = combine(near_back, (own, near), (F32, BF16), "combine_near")
    home = [mirror(far_sum), across_half(beyond_sum), beside(near_sum)]
    grad_tokens, grad_probs = pl.pallas_call(
        final_kernel,
        out_shape=[sd((rows, width), BF16), sd((top, rows), F32)],
        in_specs=[VMEM] * 4,
        out_specs=[VMEM] * 2,
        compiler_params=params(4),
        name="final",
    )(own_sum, *home)
    return grad_tokens, grad_probs.T, grad_gu, grad_down


def solution(mesh):
    groups, columns = mesh.devices.shape
    every = ("seq", "zh", "zl", "slice")
    split = Mesh(mesh.devices.reshape(groups, 2, 2, columns // 4), every)

    def spec(rank):
        return P(every, *([None] * (rank - 1)))

    return jax.shard_map(
        body,
        mesh=split,
        in_specs=(spec(2), spec(2), spec(2), spec(2), spec(4), spec(3)),
        out_specs=(spec(2), spec(2), spec(4), spec(3)),
        check_vma=False,
    )
```
